256 devices in a mesh: patch: 2 (over y_lo), theta: 32 (over z, x), phi: 4 (over y_hi, core).
Axes of the slice: x: 4, y: 4 (y_hi: 2, y_lo: 2; y = y_hi * 2 + y_lo), z: 8, core: 2. Of those that a mesh axis runs over, the one named last changes fastest.
Arguments:
- fields: float32 [2, 8, 128, 512, 128], P('patch', None, 'theta', 'phi'), may hold values from -2 to 2, as said below
- donor_base: int32 [2, 32, 4, 96], P('patch', 'theta', 'phi'), may hold values from 0 to 380
- weights: float32 [2, 32, 4, 4, 96], P('patch', 'theta', 'phi'), may hold values from 0 to 1, as said below
- frame_angle: float32 [2, 32, 4, 96], P('patch', 'theta', 'phi'), may hold values from -3.140625 to 3.140625
- destination: int32 [2, 32, 4, 96], P('patch', 'theta', 'phi'), may hold values from 0 to 127, as said below
- target_cell: int32 [2, 32, 4, 96], P('patch', 'theta', 'phi'), may hold values from 0 to 511, as said below
Outputs:
- advanced: float32 [2, 8, 128, 512, 128], P('patch', None, 'theta', 'phi')
The draws below stay inside these ranges and needn't reach their ends.
Inputs may be any that keep to these rules, and one draw needn't show every extreme that they name: `fields`: each log field has a spread of about 0.3, each vector component of about 0.5. The four weights of each border column are positive and sum to one. `destination`: only devices at the patch's edge receive: theta index 0 or 31, or phi index 0 or 3. Each device names any one device of the other patch at most 2 times; in each patch one device of the other patch is named exactly 2 times by every device. `target_cell`: every target cell lies in the outer two colatitude rows or the outer two longitude columns of its patch.
All inputs are finite; a program needn't handle non-finite values.
Results may differ from the reference program's by a relative error of at most 0.0003.
Values sent between devices are 32-bit elements; how exact they have to be, the bound alone decides.
No kernel may reach another device: no remote copies, remote signals or barrier semaphores. Data moves between devices by JAX's collectives and lax.ppermute only.
A program may use at most 64 MiB of HBM per device.

```python
import math
import jax
import jax.numpy as jnp
from jax import lax

CT = 4
CP = 128
NR = 128
SEND = 96
CAP = 2
N_THETA = 32
N_PHI = 4


def draw_fields(key, part):
    key = jax.random.fold_in(key, 11)
    scales = jnp.array([0.3, 0.5, 0.5, 0.5, 0.3, 0.5, 0.5, 0.5], jnp.float32).reshape(1, 8, 1, 1, 1)
    shape = (2, 8, CT * N_THETA, CP * N_PHI, NR)
    return jnp.clip(jax.random.normal(key, shape, jnp.float32), -4.0, 4.0) * scales


def draw_weights(key, part):
    key = jax.random.fold_in(key, 12)
    shape = (2, N_THETA, N_PHI, 4, SEND)
    raw_weight = jax.random.uniform(key, shape, jnp.float32, 0.1, 1.0)
    return raw_weight / jnp.sum(raw_weight, axis=3, keepdims=True)


def edge_devices():
    dest_count = N_THETA * N_PHI
    ids = jnp.arange(dest_count, dtype=jnp.int32)
    row_of = ids // N_PHI
    col_of = ids % N_PHI
    on_edge = (row_of == 0) | (row_of == N_THETA - 1) | (col_of == 0) | (col_of == N_PHI - 1)
    order = jnp.argsort(jnp.where(on_edge, 0, 1).astype(jnp.int32) * dest_count + ids)
    edge_count = dest_count - max(0, N_THETA - 2) * max(0, N_PHI - 2)
    return (order[:edge_count].astype(jnp.int32), edge_count)


def rim_destination(key):
    key = jax.random.fold_in(key, 13)
    dest_count = N_THETA * N_PHI
    edge_ids, edge_count = edge_devices()
    hot_key, device_key = jax.random.split(key)
    busiest = jax.random.randint(hot_key, (2,), 0, edge_count)
    device_keys = jax.random.split(device_key, 2 * dest_count)
    owners = jnp.repeat(busiest, dest_count)

    def one_device(key_one, busiest_one):
        perm_key, spot_key, order_key = jax.random.split(key_one, 3)
        targets = jax.random.permutation(perm_key, edge_count)
        targets = jnp.where(targets == busiest_one, targets[0], targets).at[0].set(busiest_one)
        spots = jax.random.permutation(spot_key, edge_count * CAP - CAP)[:SEND - CAP] + CAP
        virtual = jnp.concatenate([jnp.arange(CAP, dtype=jnp.int32), spots.astype(jnp.int32)])
        chosen = edge_ids[targets[virtual // CAP]]
        return chosen[jax.random.permutation(order_key, SEND)]
    drawn = jax.vmap(one_device)(device_keys, owners)
    return drawn.reshape(2, N_THETA, N_PHI, SEND).astype(jnp.int32)


def draw_destination(key, part):
    return rim_destination(key)


def draw_target_cell(key, part):
    receiver = rim_destination(key)
    key = jax.random.fold_in(key, 14)
    strip_key, inner_key, row_key, col_key = jax.random.split(key, 4)
    shape = receiver.shape
    dev_row = receiver // N_PHI
    dev_col = receiver % N_PHI
    usable = jnp.stack([dev_row == 0, dev_row == N_THETA - 1, dev_col == 0, dev_col == N_PHI - 1], axis=-1)
    scores = jax.random.randint(strip_key, shape + (4,), 0, 1024) * 4 + jnp.arange(4, dtype=jnp.int32)
    scores = jnp.where(usable, scores, -1)
    strip = jnp.argmax(scores, axis=-1).astype(jnp.int32)
    inner = jax.random.randint(inner_key, shape, 0, 2)
    row_any = jax.random.randint(row_key, shape, 0, CT)
    col_any = jax.random.randint(col_key, shape, 0, CP)
    row_pick = jnp.where(strip == 0, inner, jnp.where(strip == 1, CT - 2 + inner, row_any))
    col_pick = jnp.where(strip == 2, inner, jnp.where(strip == 3, CP - 2 + inner, col_any))
    return (row_pick * CP + col_pick).astype(jnp.int32)


def plant(values, own_key, low, top_value):
    spot = [jax.random.randint(jax.random.fold_in(own_key, axis), (), 0, length) for axis, length in enumerate(values.shape)]
    longest = values.shape.index(max(values.shape))
    next_to = spot[:longest] + [(spot[longest] + 1) % values.shape[longest]] + spot[longest + 1:]
    return values.at[tuple(spot)].set(low).at[tuple(next_to)].set(top_value)


def setup_inputs(seed: int = 0) -> dict:
    key_list = jax.random.split(jax.random.key(seed), 7)
    fields = draw_fields(jax.random.fold_in(key_list[6], 71), 0)
    donor_base = plant(jax.random.randint(key_list[1], (2, N_THETA, N_PHI, SEND), 0, (CT - 1) * (CP - 1)), jax.random.fold_in(key_list[1], 1), 0, ((CT - 1) * (CP - 1)) - 1).astype(jnp.int32)
    weights = draw_weights(jax.random.fold_in(key_list[6], 71), 0)
    frame_angle = jnp.clip(jax.random.uniform(key_list[3], (2, N_THETA, N_PHI, SEND), jnp.float32, -3.140625, 3.140625), -3.140625, 3.140625)
    destination = draw_destination(jax.random.fold_in(key_list[6], 71), 0)
    target_cell = draw_target_cell(jax.random.fold_in(key_list[6], 71), 0)
    return {"fields": fields, "donor_base": donor_base, "weights": weights, "frame_angle": frame_angle, "destination": destination, "target_cell": target_cell}


margin = 0.03
inner_radius = 0.35
outer_radius = 1.0
gamma_ratio = 5.0 / 3.0
gravity = 1.0
rotation = 2.0
time_step = 0.002


def stencil(far_low, near_low, near_high, far_high, spacing):
    return (far_low - 8.0 * near_low + 8.0 * near_high - far_high) / (12.0 * spacing)


def along_theta(extended, spacing):
    return stencil(extended[:, :-4, 2:-2], extended[:, 1:-3, 2:-2], extended[:, 3:-1, 2:-2], extended[:, 4:, 2:-2], spacing)


def along_phi(extended, spacing):
    return stencil(extended[:, 2:-2, :-4], extended[:, 2:-2, 1:-3], extended[:, 2:-2, 3:-1], extended[:, 2:-2, 4:], spacing)


def along_radius(centre, spacing):
    padded = jnp.pad(centre, ((0, 0), (0, 0), (0, 0), (2, 2)), mode="edge")
    return stencil(padded[..., :-4], padded[..., 1:-3], padded[..., 3:-1], padded[..., 4:], spacing)


def tendency(extended, theta_rows, phi_cols, patch_flag, theta_step, phi_step):
    shells = extended.shape[3]
    radial_step = (outer_radius - inner_radius) / shells
    radius = inner_radius + radial_step * (jnp.arange(shells, dtype=jnp.int32).astype(jnp.float32) + 0.5)
    inv_r = (1.0 / radius)[None, None, :]
    sine_theta = jnp.sin(theta_rows)[:, None, None]
    cosine_theta = jnp.cos(theta_rows)[:, None, None]
    cot_theta = cosine_theta / sine_theta
    sine_phi = jnp.sin(phi_cols)[None, :, None]
    cosine_phi = jnp.cos(phi_cols)[None, :, None]
    centre = extended[:, 2:-2, 2:-2]
    grad_r = along_radius(centre, radial_step)
    grad_t = along_theta(extended, theta_step) * inv_r
    grad_p = along_phi(extended, phi_step) * (inv_r / sine_theta)
    log_rho, vel_r, vel_t, vel_p, log_p, mag_r, mag_t, mag_p = [centre[which] for which in range(8)]

    def advect(which):
        return vel_r * grad_r[which] + vel_t * grad_t[which] + vel_p * grad_p[which]

    diverge = grad_r[1] + 2.0 * vel_r * inv_r + grad_t[2] + cot_theta * vel_t * inv_r + grad_p[3]
    cur_r = grad_t[7] + cot_theta * mag_p * inv_r - grad_p[6]
    cur_t = grad_p[5] - grad_r[7] - mag_p * inv_r
    cur_p = grad_r[6] + mag_t * inv_r - grad_t[5]
    electric = jnp.stack([
        extended[2] * extended[7] - extended[3] * extended[6],
        extended[3] * extended[5] - extended[1] * extended[7],
        extended[1] * extended[6] - extended[2] * extended[5]])
    elec_centre = electric[:, 2:-2, 2:-2]
    elec_r = along_radius(elec_centre, radial_step)
    elec_t = along_theta(electric, theta_step) * inv_r
    elec_p = along_phi(electric, phi_step) * (inv_r / sine_theta)
    induce_r = elec_t[2] + cot_theta * elec_centre[2] * inv_r - elec_p[1]
    induce_t = elec_p[0] - elec_r[2] - elec_centre[2] * inv_r
    induce_p = elec_r[1] + elec_centre[1] * inv_r - elec_t[0]
    omega_y = rotation * patch_flag
    omega_z = rotation * (1.0 - patch_flag)
    omega_r = omega_y * sine_theta * sine_phi + omega_z * cosine_theta
    omega_t = omega_y * cosine_theta * sine_phi - omega_z * sine_theta
    omega_p = omega_y * cosine_phi
    inv_rho = jnp.exp(-log_rho)
    temper = jnp.exp(log_p - log_rho)
    rate_rho = -advect(0) - diverge
    rate_p = -advect(4) - gamma_ratio * diverge
    rate_vr = (-advect(1) + (vel_t * vel_t + vel_p * vel_p) * inv_r - temper * grad_r[4]
               + inv_rho * (cur_t * mag_p - cur_p * mag_t)
               - 2.0 * (omega_t * vel_p - omega_p * vel_t) - gravity * inv_r * inv_r)
    rate_vt = (-advect(2) - (vel_r * vel_t - cot_theta * vel_p * vel_p) * inv_r - temper * grad_t[4]
               + inv_rho * (cur_p * mag_r - cur_r * mag_p)
               - 2.0 * (omega_p * vel_r - omega_r * vel_p))
    rate_vp = (-advect(3) - (vel_r * vel_p + cot_theta * vel_t * vel_p) * inv_r - temper * grad_p[4]
               + inv_rho * (cur_r * mag_t - cur_t * mag_r)
               - 2.0 * (omega_r * vel_t - omega_t * vel_r))
    return jnp.stack([rate_rho, rate_vr, rate_vt, rate_vp, rate_p, induce_r, induce_t, induce_p])


def rotate(values, cosine, sine):
    new_vt = cosine * values[2] - sine * values[3]
    new_vp = sine * values[2] + cosine * values[3]
    new_bt = cosine * values[6] - sine * values[7]
    new_bp = sine * values[6] + cosine * values[7]
    return jnp.stack([values[0], values[1], new_vt, new_vp, values[4], values[5], new_bt, new_bp])


def patch_tendency(fields_patch, patch_flag):
    rows_total = CT * N_THETA
    cols_total = CP * N_PHI
    theta_step = (0.5 * math.pi + 2.0 * margin) / rows_total
    phi_step = (1.5 * math.pi + 2.0 * margin) / cols_total
    phi_cols = -0.75 * math.pi - margin + (jnp.arange(cols_total, dtype=jnp.int32).astype(jnp.float32) + 0.5) * phi_step
    padded = jnp.pad(fields_patch, ((0, 0), (2, 2), (2, 2), (0, 0)))

    def one_block(block_index):
        row_start = (block_index * CT).astype(jnp.int32)
        extended = lax.dynamic_slice_in_dim(padded, row_start, CT + 4, 1)
        row_index = row_start + jnp.arange(CT, dtype=jnp.int32)
        theta_rows = 0.25 * math.pi - margin + (row_index.astype(jnp.float32) + 0.5) * theta_step
        return tendency(extended, theta_rows, phi_cols, patch_flag, theta_step, phi_step)

    blocks = lax.map(one_block, jnp.arange(N_THETA, dtype=jnp.int32))
    return jnp.moveaxis(blocks, 0, 1).reshape(8, rows_total, cols_total, NR)


def advance(fields):
    return jnp.stack([patch_tendency(fields[0], 0.0), patch_tendency(fields[1], 1.0)])


def overset(updated, donor_base, weights, frame_angle, destination, target_cell):
    rows_total = CT * N_THETA
    cols_total = CP * N_PHI
    slot_count = N_THETA * N_PHI * SEND
    flat_fields = updated.reshape(2, 8, rows_total * cols_total, NR)
    dev_row = jnp.arange(N_THETA, dtype=jnp.int32)[:, None, None]
    dev_col = jnp.arange(N_PHI, dtype=jnp.int32)[None, :, None]
    results = []
    for receiver in range(2):
        donor_patch = 1 - receiver
        corner_base = donor_base[donor_patch]
        corner = ((dev_row * CT + corner_base // (CP - 1)) * cols_total + dev_col * CP + corner_base % (CP - 1)).reshape(slot_count)
        weight_rows = jnp.transpose(weights[donor_patch], (2, 0, 1, 3)).reshape(4, slot_count)
        source = flat_fields[donor_patch]
        donor_value = weight_rows[0][None, :, None] * jnp.take(source, corner, axis=1)
        donor_value = donor_value + weight_rows[1][None, :, None] * jnp.take(source, corner + 1, axis=1)
        donor_value = donor_value + weight_rows[2][None, :, None] * jnp.take(source, corner + cols_total, axis=1)
        donor_value = donor_value + weight_rows[3][None, :, None] * jnp.take(source, corner + cols_total + 1, axis=1)
        angle_flat = frame_angle[donor_patch].reshape(slot_count)
        donor_value = rotate(donor_value, jnp.cos(angle_flat)[:, None], jnp.sin(angle_flat)[:, None])
        receiver_dev = destination[donor_patch].reshape(slot_count)
        cell_ids = target_cell[donor_patch].reshape(slot_count)
        target = ((receiver_dev // N_PHI) * CT + cell_ids // CP) * cols_total + (receiver_dev % N_PHI) * CP + cell_ids % CP
        summed = jnp.zeros((8, rows_total * cols_total, NR), jnp.float32).at[:, target, :].add(donor_value)
        counts = jnp.zeros((rows_total * cols_total,), jnp.float32).at[target].add(1.0)
        merged = jnp.where(counts[None, :, None] > 0.0, summed / counts[None, :, None], flat_fields[receiver])
        results.append(merged.reshape(8, rows_total, cols_total, NR))
    return jnp.stack(results)


def reference(fields, donor_base, weights, frame_angle, destination, target_cell):
    section_one = fields + time_step * advance(fields)
    section_one = overset(section_one, donor_base, weights, frame_angle, destination, target_cell)
    section_two = 0.5 * (fields + section_one + time_step * advance(section_one))
    return overset(section_two, donor_base, weights, frame_angle, destination, target_cell)
```

```python
import math

import jax
import jax.numpy as jnp
from jax import lax
from jax.experimental import pallas as pl
from jax.experimental.pallas import tpu as pltpu
from jax.sharding import PartitionSpec as P

margin = 0.03
inner_radius = 0.35
outer_radius = 1.0
gamma_ratio = 5.0 / 3.0
gravity = 1.0
rotation = 2.0
time_step = 0.002

ROWS, COLS, SHELLS, FIELDS, SLOTS = 4, 128, 128, 8, 96
CELLS = ROWS * COLS
N_THETA, N_PHI = 32, 4
DEVS = N_THETA * N_PHI
CAPACITY = 2
PAD = 8
EXT = COLS + 2 * PAD
THETA_STEP = (0.5 * math.pi + 2.0 * margin) / (ROWS * N_THETA)
PHI_STEP = (1.5 * math.pi + 2.0 * margin) / (COLS * N_PHI)
RADIAL_STEP = (outer_radius - inner_radius) / SHELLS
VMEM = pl.BlockSpec(memory_space=pltpu.VMEM)
SMEM = pl.BlockSpec(memory_space=pltpu.SMEM)


def diff(far_low, near_low, near_high, far_high):
    return (far_low - far_high) + 8.0 * (near_high - near_low)


def step_kernel(second, *refs):
    if second:
        base, refs = refs[0], refs[1:]
    own, above, below, left, right, row_const, phi_const, inv_r_ref, corner, angle, place, updated, send, ext, donor = refs

    for i in range(ROWS):
        for f in range(FIELDS):
            ext[f, i, PAD : PAD + COLS, :] = own[f, i]
            ext[f, i, PAD - 2 : PAD, :] = left[f, i]
            ext[f, i, PAD + COLS : PAD + COLS + 2, :] = right[f, i]

    lane = lax.broadcasted_iota(jnp.int32, (8, SHELLS), 1)
    first, second_lane = lane < 1, lane < 2
    last, before_last = lane > SHELLS - 2, lane > SHELLS - 3
    inv_r = inv_r_ref[...]
    k_r = 1.0 / (12.0 * RADIAL_STEP)
    g_t = inv_r * (1.0 / (12.0 * THETA_STEP))

    def d_r(x):
        near_low = jnp.where(first, x, pltpu.roll(x, 1, 1))
        far_low = jnp.where(second_lane, near_low, pltpu.roll(x, 2, 1))
        near_high = jnp.where(last, x, pltpu.roll(x, SHELLS - 1, 1))
        far_high = jnp.where(before_last, near_high, pltpu.roll(x, SHELLS - 2, 1))
        return diff(far_low, near_low, near_high, far_high) * k_r

    def plane(i):
        if i < 0:
            return above, i + 2
        if i >= ROWS:
            return below, i - ROWS
        return own, i

    for i in range(ROWS):
        sine, cosine, cot, inv_sine = [row_const[i, k] for k in range(4)]
        omega_y, omega_z = row_const[i, 4], row_const[i, 5]
        g_p = inv_r * (inv_sine * (1.0 / (12.0 * PHI_STEP)))
        cot_r = inv_r * cot

        def tile(j, carry):
            start = pl.multiple_of(j * 8, 8)
            rows = pl.ds(start, 8)
            q, ur, ut, up, h, br, bt, bp = [own[f, i, rows, :] for f in range(FIELDS)]
            near = []
            for d in (-2, -1, 1, 2):
                ref, p = plane(i + d)
                near.append([ref[f, p, rows, :] for f in range(FIELDS)])
            tq, tur, tut, tup, th, tbr, _, tbp = [
                diff(*[n[f] for n in near]) * g_t if f != 6 else None for f in range(FIELDS)
            ]
            t_er = diff(*[n[2] * n[7] - n[3] * n[6] for n in near]) * g_t
            t_ep = diff(*[n[1] * n[6] - n[2] * n[5] for n in near]) * g_t
            near = []
            for d in (-2, -1, 1, 2):
                near.append([ext[f, i, pl.ds(start + (PAD + d), 8), :] for f in range(FIELDS)])
            pq, pur, put, pup, ph, pbr, pbt, _ = [
                diff(*[n[f] for n in near]) * g_p if f != 7 else None for f in range(FIELDS)
            ]
            p_er = diff(*[n[2] * n[7] - n[3] * n[6] for n in near]) * g_p
            p_et = diff(*[n[3] * n[5] - n[1] * n[7] for n in near]) * g_p
            er = ut * bp - up * bt
            et = up * br - ur * bp
            ep = ur * bt - ut * br
            rq, rur, rut, rup, rh, rbt, rbp, r_et, r_ep = [d_r(x) for x in (q, ur, ut, up, h, bt, bp, et, ep)]

            div = rur + 2.0 * ur * inv_r + tut + cot_r * ut + pup
            cur_r = tbp + cot_r * bp - pbt
            cur_t = pbr - rbp - bp * inv_r
            cur_p = rbt + bt * inv_r - tbr
            sin_phi = phi_const[0, rows, :]
            cos_phi = phi_const[1, rows, :]
            w_r = (omega_y * sine) * sin_phi + omega_z * cosine
            w_t = (omega_y * cosine) * sin_phi - omega_z * sine
            w_p = omega_y * cos_phi
            inv_rho = jnp.exp(-q)
            temper = jnp.exp(h - q)

            def adv(gr, gt, gp):
                return ur * gr + ut * gt + up * gp

            rates = [
                -adv(rq, tq, pq) - div,
                -adv(rur, tur, pur)
                + (ut * ut + up * up) * inv_r
                - temper * rh
                + inv_rho * (cur_t * bp - cur_p * bt)
                - 2.0 * (w_t * up - w_p * ut)
                - gravity * inv_r * inv_r,
                -adv(rut, tut, put)
                - (ur * ut * inv_r - cot_r * (up * up))
                - temper * th
                + inv_rho * (cur_p * br - cur_r * bp)
                - 2.0 * (w_p * ur - w_r * up),
                -adv(rup, tup, pup)
                - (ur * up * inv_r + cot_r * (ut * up))
                - temper * ph
                + inv_rho * (cur_r * bt - cur_t * br)
                - 2.0 * (w_r * ut - w_t * ur),
                -adv(rh, th, ph) - gamma_ratio * div,
                t_ep + cot_r * ep - p_et,
                p_er - r_ep - ep * inv_r,
                r_et + et * inv_r - t_er,
            ]
            centre = [q, ur, ut, up, h, br, bt, bp]
            for f in range(FIELDS):
                if second:
                    new = 0.5 * (base[f, i, rows, :] + centre[f] + time_step * rates[f])
                else:
                    new = centre[f] + time_step * rates[f]
                updated[f, i, rows, :] = new
            return carry

        lax.fori_loop(0, COLS // 8, tile, 0)

    values = [
        jnp.dot(
            corner[...],
            updated[f].reshape(CELLS, SHELLS),
            precision=lax.Precision.HIGHEST,
            preferred_element_type=jnp.float32,
        )
        for f in range(FIELDS)
    ]
    c, s = angle[0], angle[1]
    for t, p in ((2, 3), (6, 7)):
        values[t], values[p] = c * values[t] - s * values[p], s * values[t] + c * values[p]
    donor[...] = jnp.swapaxes(jnp.stack(values), 0, 1)
    send[...] = jnp.zeros_like(send)

    def put(m, carry):
        send[place[m]] = donor[m]
        return carry

    lax.fori_loop(0, SLOTS, put, 0)


def merge_kernel(updated, moved, pick, mean, other, merged, gathered):
    start = other[0] * (DEVS * CAPACITY)
    gathered[...] = jnp.swapaxes(moved[pl.ds(start, DEVS * CAPACITY)], 0, 1)
    weight = mean[...]
    for f in range(FIELDS):
        v = gathered[f]
        high = v.astype(jnp.bfloat16)
        rest = v - high.astype(jnp.float32)
        middle = rest.astype(jnp.bfloat16)
        low = (rest - middle.astype(jnp.float32)).astype(jnp.bfloat16)
        total = sum(
            jnp.dot(pick[...], x, preferred_element_type=jnp.float32) for x in (low, middle, high)
        )
        kept = updated[f].reshape(CELLS, SHELLS)
        merged[f] = jnp.where(weight > 0.0, total * weight, kept).reshape(ROWS, COLS, SHELLS)


def params():
    return pltpu.CompilerParams(vmem_limit_bytes=48 * 1024 * 1024)


def run_step(second, args):
    return pl.pallas_call(
        lambda *refs: step_kernel(second, *refs),
        out_shape=(
            jax.ShapeDtypeStruct((FIELDS, ROWS, COLS, SHELLS), jnp.float32),
            jax.ShapeDtypeStruct((2 * DEVS * CAPACITY, FIELDS, SHELLS), jnp.float32),
        ),
        in_specs=[VMEM] * (6 if second else 5) + [SMEM] + [VMEM] * 4 + [SMEM],
        out_specs=(VMEM, VMEM),
        scratch_shapes=[
            pltpu.VMEM((FIELDS, ROWS, EXT, SHELLS), jnp.float32),
            pltpu.VMEM((SLOTS, FIELDS, SHELLS), jnp.float32),
        ],
        compiler_params=params(),
    )(*args)


def run_merge(*args):
    return pl.pallas_call(
        merge_kernel,
        out_shape=jax.ShapeDtypeStruct((FIELDS, ROWS, COLS, SHELLS), jnp.float32),
        in_specs=[VMEM] * 4 + [SMEM],
        out_specs=VMEM,
        scratch_shapes=[pltpu.VMEM((FIELDS, DEVS * CAPACITY, SHELLS), jnp.float32)],
        compiler_params=params(),
    )(*args)


def halos(x):
    up = [(i, i + 1) for i in range(N_THETA - 1)]
    down = [(j, i) for i, j in up]
    right = [(i, i + 1) for i in range(N_PHI - 1)]
    left = [(j, i) for i, j in right]
    above = lax.ppermute(x[:, ROWS - 2 :], "theta", up)
    below = lax.ppermute(x[:, :2], "theta", down)
    before = lax.ppermute(x[:, :, COLS - 2 :], "phi", right)
    after = lax.ppermute(x[:, :, :2], "phi", left)
    return above, below, before, after


def local(fields, donor_base, weights, frame_angle, destination, target_cell):
    own = fields[0]
    patch = lax.axis_index("patch")
    other = 1 - patch

    row_index = lax.axis_index("theta") * ROWS + jnp.arange(ROWS, dtype=jnp.int32)
    theta = 0.25 * math.pi - margin + (row_index.astype(jnp.float32) + 0.5) * THETA_STEP
    col_index = lax.axis_index("phi") * COLS + jnp.arange(COLS, dtype=jnp.int32)
    phi = -0.75 * math.pi - margin + (col_index.astype(jnp.float32) + 0.5) * PHI_STEP
    flag = patch.astype(jnp.float32)
    sine, cosine = jnp.sin(theta), jnp.cos(theta)
    ones = jnp.ones_like(sine)
    row_const = jnp.stack(
        [sine, cosine, cosine / sine, 1.0 / sine, ones * (rotation * flag), ones * (rotation * (1.0 - flag))], axis=1
    )
    phi_const = jnp.broadcast_to(jnp.stack([jnp.sin(phi), jnp.cos(phi)])[:, :, None], (2, COLS, SHELLS))
    radius = inner_radius + RADIAL_STEP * (jnp.arange(SHELLS, dtype=jnp.int32).astype(jnp.float32) + 0.5)
    inv_r = jnp.broadcast_to((1.0 / radius)[None, :], (8, SHELLS))

    base = donor_base[0, 0, 0]
    first = base // (COLS - 1) * COLS + base % (COLS - 1)
    w = weights[0, 0, 0]
    cells = jnp.arange(CELLS, dtype=jnp.int32)[None, :]
    corner = sum(
        jnp.where(cells == (first + offset)[:, None], w[k][:, None], 0.0)
        for k, offset in enumerate((0, 1, COLS, COLS + 1))
    )
    angle = frame_angle[0, 0, 0]
    angle = jnp.broadcast_to(jnp.stack([jnp.cos(angle), jnp.sin(angle)])[:, :, None], (2, SLOTS, SHELLS))
    receiver = destination[0, 0, 0]
    slot = jnp.arange(SLOTS, dtype=jnp.int32)
    rank = jnp.sum(
        ((receiver[:, None] == receiver[None, :]) & (slot[None, :] < slot[:, None])).astype(jnp.int32), axis=1
    )
    place = (other * DEVS + receiver) * CAPACITY + rank
    position = jnp.arange(2 * DEVS * CAPACITY, dtype=jnp.int32)
    cell_ids = target_cell[0, 0, 0]
    sent_ids = jnp.sum(jnp.where(position[:, None] == place[None, :], cell_ids[None, :] + 1, 0), axis=1) - 1
    sent_ids = jnp.broadcast_to(sent_ids.reshape(2 * DEVS, CAPACITY, 1), (2 * DEVS, CAPACITY, SHELLS))
    everyone = ("patch", "theta", "phi")
    got_ids = lax.all_to_all(sent_ids, everyone, 0, 0, tiled=True)[:, :, 0].reshape(2, DEVS * CAPACITY)
    got_ids = lax.dynamic_index_in_dim(got_ids, other, 0, keepdims=False)
    picked = got_ids[None, :] == jnp.arange(CELLS, dtype=jnp.int32)[:, None]
    pick = picked.astype(jnp.bfloat16)
    count = jnp.sum(picked.astype(jnp.float32), axis=1)
    mean = jnp.where(count > 0.0, 1.0 / jnp.maximum(count, 1.0), 0.0)
    mean = jnp.broadcast_to(mean[:, None], (CELLS, SHELLS))
    other_ref = other.astype(jnp.int32).reshape(1)

    def overset(updated, send):
        send = send.reshape(2 * DEVS, CAPACITY * FIELDS, SHELLS)
        moved = lax.all_to_all(send, everyone, 0, 0, tiled=True)
        moved = moved.reshape(2 * DEVS * CAPACITY, FIELDS, SHELLS)
        return run_merge(updated, moved, pick, mean, other_ref)

    tail = (row_const, phi_const, inv_r, corner, angle, place)
    one = overset(*run_step(False, (own, *halos(own), *tail)))
    two = overset(*run_step(True, (own, one, *halos(one), *tail)))
    return two[None]


def solution(mesh):
    placed = (
        P("patch", None, "theta", "phi", None),
        P("patch", "theta", "phi", None),
        P("patch", "theta", "phi", None, None),
        P("patch", "theta", "phi", None),
        P("patch", "theta", "phi", None),
        P("patch", "theta", "phi", None),
    )
    return jax.shard_map(
        local,
        mesh=mesh,
        in_specs=placed,
        out_specs=P("patch", None, "theta", "phi", None),
        check_vma=False,
    )
```

```python
import math

import jax
import jax.numpy as jnp
from jax import lax
from jax.experimental import pallas as pl
from jax.experimental.pallas import tpu as pltpu
from jax.sharding import PartitionSpec as P

margin = 0.03
inner_radius = 0.35
outer_radius = 1.0
gamma_ratio = 5.0 / 3.0
gravity = 1.0
rotation = 2.0
time_step = 0.002

ROWS, COLS, SHELLS, FIELDS, SLOTS = 4, 128, 128, 8, 96
HALF = ROWS // 2
CELLS = ROWS * COLS
N_THETA, N_PHI = 32, 4
DEVS = N_THETA * N_PHI
PAD = 8
EXT = COLS + 2 * PAD
THETA_STEP = (0.5 * math.pi + 2.0 * margin) / (ROWS * N_THETA)
PHI_STEP = (1.5 * math.pi + 2.0 * margin) / (COLS * N_PHI)
RADIAL_STEP = (outer_radius - inner_radius) / SHELLS
VMEM = pl.BlockSpec(memory_space=pltpu.VMEM)
SMEM = pl.BlockSpec(memory_space=pltpu.SMEM)
ANY = pl.BlockSpec(memory_space=pl.ANY)
EVERYONE = ("patch", "theta", "phi")


def struct(*shape):
    return jax.ShapeDtypeStruct(shape, jnp.float32)


HALF_BLOCK = (FIELDS, HALF, COLS, SHELLS)
RIM = (FIELDS, 8, SHELLS)


def params(mib):
    return pltpu.CompilerParams(vmem_limit_bytes=mib * 1024 * 1024)


def store_rims(top, bottom, west, east):
    for f in range(FIELDS):
        for i in range(ROWS):
            ref = (top, bottom)[i // HALF]
            west[f, 2 * i : 2 * i + 2, :] = ref[f, i % HALF, :2, :]
            east[f, 2 * i : 2 * i + 2, :] = ref[f, i % HALF, COLS - 2 :, :]


def split_kernel(fields, top, bottom, west, east, sems):
    copies = [
        pltpu.make_async_copy(fields.at[:, :HALF], top, sems.at[0]),
        pltpu.make_async_copy(fields.at[:, HALF:], bottom, sems.at[1]),
    ]
    for copy in copies:
        copy.start()
    for copy in copies:
        copy.wait()
    store_rims(top, bottom, west, east)


def run_split(fields):
    return pl.pallas_call(
        split_kernel,
        out_shape=(struct(*HALF_BLOCK), struct(*HALF_BLOCK), struct(*RIM), struct(*RIM)),
        in_specs=[ANY],
        out_specs=(VMEM,) * 4,
        scratch_shapes=[pltpu.SemaphoreType.DMA((2,))],
        compiler_params=params(16),
    )(fields)


def diff(far_low, near_low, near_high, far_high):
    return (far_low - far_high) + 8.0 * (near_high - near_low)


def step_kernel(second, *refs):
    if second:
        base_hbm, fix_above, fix_below, *refs = refs
    (
        top, bottom, above, below, before, after, edge, row_const, phi_const, inv_r_ref, corner, angle, place,
        new_top, new_bottom, send, ext, donor, base, sems,
    ) = refs
    inside = pl.ds(PAD, COLS)
    copies = [
        pltpu.make_async_copy(ref, ext.at[:, start : start + HALF, inside], sems.at[n])
        for n, (ref, start) in enumerate(((above, 0), (top, 2), (bottom, 4), (below, 6)))
    ]
    if second:
        copies.append(pltpu.make_async_copy(base_hbm, base, sems.at[4]))
    for copy in copies:
        copy.start()
    send[...] = jnp.zeros_like(send)
    west_edge, east_edge = edge[2] > 0, edge[3] > 0
    for f in range(FIELDS):
        for i in range(ROWS):
            pair = slice(2 * i, 2 * i + 2)
            ext[f, 2 + i, PAD - 2 : PAD, :] = jnp.where(west_edge, 0.0, before[f, pair, :])
            ext[f, 2 + i, PAD + COLS : PAD + COLS + 2, :] = jnp.where(east_edge, 0.0, after[f, pair, :])
    for copy in copies:
        copy.wait()
    if second:
        for f in range(FIELDS):
            for i in range(HALF):
                for start, ref in ((0, fix_above), (6, fix_below)):
                    ext[f, start + i, PAD : PAD + 2, :] = ref[f, 4 * i : 4 * i + 2, :]
                    ext[f, start + i, PAD + COLS - 2 : PAD + COLS, :] = ref[f, 4 * i + 2 : 4 * i + 4, :]

    @pl.when(edge[0] > 0)
    def _():
        ext[:, 0:HALF] = jnp.zeros((FIELDS, HALF, EXT, SHELLS), jnp.float32)

    @pl.when(edge[1] > 0)
    def _():
        ext[:, 6 : 6 + HALF] = jnp.zeros((FIELDS, HALF, EXT, SHELLS), jnp.float32)

    lane = lax.broadcasted_iota(jnp.int32, (8, SHELLS), 1)
    first, second_lane = lane < 1, lane < 2
    last, before_last = lane > SHELLS - 2, lane > SHELLS - 3
    inv_r = inv_r_ref[...]
    k_r = 1.0 / (12.0 * RADIAL_STEP)
    g_t = inv_r * (1.0 / (12.0 * THETA_STEP))

    def d_r(x):
        near_low = jnp.where(first, x, pltpu.roll(x, 1, 1))
        far_low = jnp.where(second_lane, near_low, pltpu.roll(x, 2, 1))
        near_high = jnp.where(last, x, pltpu.roll(x, SHELLS - 1, 1))
        far_high = jnp.where(before_last, near_high, pltpu.roll(x, SHELLS - 2, 1))
        return diff(far_low, near_low, near_high, far_high) * k_r

    for i in range(ROWS):
        sine, cosine, cot, inv_sine = [row_const[i, k] for k in range(4)]
        omega_y, omega_z = row_const[i, 4], row_const[i, 5]
        g_p = inv_r * (inv_sine * (1.0 / (12.0 * PHI_STEP)))
        cot_r = inv_r * cot
        out = (new_top, new_bottom)[i // HALF]

        def tile(j, carry):
            start = pl.multiple_of(j * 8, 8)
            rows = pl.ds(start, 8)
            padded = pl.ds(pl.multiple_of(start + PAD, 8), 8)
            q, ur, ut, up, h, br, bt, bp = [ext[f, 2 + i, padded, :] for f in range(FIELDS)]
            near = [[ext[f, 2 + i + d, padded, :] for f in range(FIELDS)] for d in (-2, -1, 1, 2)]
            tq, tur, tut, tup, th, tbr, _, tbp = [
                diff(*[n[f] for n in near]) * g_t if f != 6 else None for f in range(FIELDS)
            ]
            t_er = diff(*[n[2] * n[7] - n[3] * n[6] for n in near]) * g_t
            t_ep = diff(*[n[1] * n[6] - n[2] * n[5] for n in near]) * g_t
            near = [[ext[f, 2 + i, pl.ds(start + (PAD + d), 8), :] for f in range(FIELDS)] for d in (-2, -1, 1, 2)]
            pq, pur, put, pup, ph, pbr, pbt, _ = [
                diff(*[n[f] for n in near]) * g_p if f != 7 else None for f in range(FIELDS)
            ]
            p_er = diff(*[n[2] * n[7] - n[3] * n[6] for n in near]) * g_p
            p_et = diff(*[n[3] * n[5] - n[1] * n[7] for n in near]) * g_p
            er = ut * bp - up * bt
            et = up * br - ur * bp
            ep = ur * bt - ut * br
            rq, rur, rut, rup, rh, rbt, rbp, r_et, r_ep = [d_r(x) for x in (q, ur, ut, up, h, bt, bp, et, ep)]

            div = rur + 2.0 * ur * inv_r + tut + cot_r * ut + pup
            cur_r = tbp + cot_r * bp - pbt
            cur_t = pbr - rbp - bp * inv_r
            cur_p = rbt + bt * inv_r - tbr
            sin_phi = phi_const[0, rows, :]
            cos_phi = phi_const[1, rows, :]
            w_r = (omega_y * sine) * sin_phi + omega_z * cosine
            w_t = (omega_y * cosine) * sin_phi - omega_z * sine
            w_p = omega_y * cos_phi
            inv_rho = jnp.exp(-q)
            temper = jnp.exp(h - q)

            def adv(gr, gt, gp):
                return ur * gr + ut * gt + up * gp

            rates = [
                -adv(rq, tq, pq) - div,
                -adv(rur, tur, pur)
                + (ut * ut + up * up) * inv_r
                - temper * rh
                + inv_rho * (cur_t * bp - cur_p * bt)
                - 2.0 * (w_t * up - w_p * ut)
                - gravity * inv_r * inv_r,
                -adv(rut, tut, put)
                - (ur * ut * inv_r - cot_r * (up * up))
                - temper * th
                + inv_rho * (cur_p * br - cur_r * bp)
                - 2.0 * (w_p * ur - w_r * up),
                -adv(rup, tup, pup)
                - (ur * up * inv_r + cot_r * (ut * up))
                - temper * ph
                + inv_rho * (cur_r * bt - cur_t * br)
                - 2.0 * (w_r * ut - w_t * ur),
                -adv(rh, th, ph) - gamma_ratio * div,
                t_ep + cot_r * ep - p_et,
                p_er - r_ep - ep * inv_r,
                r_et + et * inv_r - t_er,
            ]
            centre = [q, ur, ut, up, h, br, bt, bp]
            for f in range(FIELDS):
                if second:
                    new = 0.5 * (base[f, i, rows, :] + centre[f] + time_step * rates[f])
                else:
                    new = centre[f] + time_step * rates[f]
                out[f, i % HALF, rows, :] = new
            return carry

        lax.fori_loop(0, COLS // 8, tile, 0)

    def product(f):
        total = None
        for n, ref in enumerate((new_top, new_bottom)):
            part = jnp.dot(
                corner[:, n * HALF * COLS : (n + 1) * HALF * COLS],
                ref[f].reshape(HALF * COLS, SHELLS),
                precision=lax.Precision.HIGHEST,
                preferred_element_type=jnp.float32,
            )
            total = part if total is None else total + part
        return total

    values = [product(f) for f in range(FIELDS)]
    c, s = angle[0], angle[1]
    for t, p in ((2, 3), (6, 7)):
        values[t], values[p] = c * values[t] - s * values[p], s * values[t] + c * values[p]
    donor[...] = jnp.swapaxes(jnp.stack(values), 0, 1)

    def put(m, carry):
        for k in range(8):
            send[place[8 * m + k]] = donor[8 * m + k]
        return carry

    lax.fori_loop(0, SLOTS // 8, put, 0)


def run_step(second, args):
    return pl.pallas_call(
        lambda *refs: step_kernel(second, *refs),
        out_shape=(struct(*HALF_BLOCK), struct(*HALF_BLOCK), struct(2 * DEVS, FIELDS, SHELLS)),
        in_specs=([ANY, VMEM, VMEM] if second else []) + [VMEM] * 6 + [SMEM] * 2 + [VMEM] * 4 + [SMEM],
        out_specs=(VMEM,) * 3,
        scratch_shapes=[
            pltpu.VMEM((FIELDS, ROWS + 4, EXT, SHELLS), jnp.float32),
            pltpu.VMEM((SLOTS, FIELDS, SHELLS), jnp.float32),
            pltpu.VMEM((FIELDS, ROWS if second else 1, COLS, SHELLS), jnp.float32),
            pltpu.SemaphoreType.DMA((5,)),
        ],
        compiler_params=params(24),
    )(*args)


def merge_kernel(last, top, bottom, direct, mate, early, late, pick, mean, edge, *refs):
    if last:
        merged, gathered = refs
    else:
        new_top, new_bottom, west, east, head, foot, gathered = refs
    gathered[:, :DEVS, :] = jnp.swapaxes(direct[...], 0, 1)
    on_edge = edge[0] + edge[1] > 0

    @pl.when(on_edge)
    def _():
        gathered[:, DEVS : DEVS + DEVS // 2, :] = jnp.swapaxes(early[...], 0, 1)
        gathered[:, DEVS + DEVS // 2 :, :] = jnp.swapaxes(late[...], 0, 1)

    @pl.when(jnp.logical_not(on_edge))
    def _():
        gathered[:, DEVS:, :] = jnp.swapaxes(mate[...], 0, 1)

    weight = mean[...]
    for f in range(FIELDS):
        v = gathered[f]
        high = v.astype(jnp.bfloat16)
        rest = v - high.astype(jnp.float32)
        middle = rest.astype(jnp.bfloat16)
        low = (rest - middle.astype(jnp.float32)).astype(jnp.bfloat16)
        total = sum(jnp.dot(pick[...], x, preferred_element_type=jnp.float32) for x in (low, middle, high))
        for n, ref in enumerate((top, bottom)):
            part = slice(n * HALF * COLS, (n + 1) * HALF * COLS)
            kept = ref[f].reshape(HALF * COLS, SHELLS)
            result = jnp.where(weight[part] > 0.0, total[part] * weight[part], kept).reshape(HALF, COLS, SHELLS)
            if last:
                merged[f, n * HALF : (n + 1) * HALF] = result
            else:
                (new_top, new_bottom)[n][f] = result
    if not last:
        store_rims(new_top, new_bottom, west, east)
        for f in range(FIELDS):
            for i in range(HALF):
                for ref, fix in ((new_top, head), (new_bottom, foot)):
                    fix[f, 4 * i : 4 * i + 2, :] = ref[f, i, :2, :]
                    fix[f, 4 * i + 2 : 4 * i + 4, :] = ref[f, i, COLS - 2 :, :]


def run_merge(last, *args):
    if last:
        shapes = (struct(FIELDS, ROWS, COLS, SHELLS),)
    else:
        shapes = (struct(*HALF_BLOCK),) * 2 + (struct(*RIM),) * 4
    return pl.pallas_call(
        lambda *refs: merge_kernel(last, *refs),
        out_shape=shapes,
        in_specs=[VMEM] * 8 + [SMEM],
        out_specs=(VMEM,) * len(shapes),
        scratch_shapes=[pltpu.VMEM((FIELDS, 2 * DEVS, SHELLS), jnp.float32)],
        compiler_params=params(16),
    )(*args)


def shift(x, axis, size, by):
    return lax.ppermute(x, axis, [(i, (i + by) % size) for i in range(size)])


def local(fields, donor_base, weights, frame_angle, destination, target_cell):
    own = fields[0]
    patch, ti, pi = [lax.axis_index(axis) for axis in EVERYONE]
    other = 1 - patch

    top, bottom, west, east = run_split(own)
    above, below = shift(bottom, "theta", N_THETA, 1), shift(top, "theta", N_THETA, -1)
    before, after = shift(east, "phi", N_PHI, 1), shift(west, "phi", N_PHI, -1)
    edge = jnp.stack([ti == 0, ti == N_THETA - 1, pi == 0, pi == N_PHI - 1]).astype(jnp.int32)

    row_index = ti * ROWS + jnp.arange(ROWS, dtype=jnp.int32)
    theta = 0.25 * math.pi - margin + (row_index.astype(jnp.float32) + 0.5) * THETA_STEP
    col_index = pi * COLS + jnp.arange(COLS, dtype=jnp.int32)
    phi = -0.75 * math.pi - margin + (col_index.astype(jnp.float32) + 0.5) * PHI_STEP
    flag = patch.astype(jnp.float32)
    sine, cosine = jnp.sin(theta), jnp.cos(theta)
    ones = jnp.ones_like(sine)
    row_const = jnp.stack(
        [sine, cosine, cosine / sine, 1.0 / sine, ones * (rotation * flag), ones * (rotation * (1.0 - flag))], axis=1
    )
    phi_const = jnp.broadcast_to(jnp.stack([jnp.sin(phi), jnp.cos(phi)])[:, :, None], (2, COLS, SHELLS))
    radius = inner_radius + RADIAL_STEP * (jnp.arange(SHELLS, dtype=jnp.int32).astype(jnp.float32) + 0.5)
    inv_r = jnp.broadcast_to((1.0 / radius)[None, :], (8, SHELLS))

    base = donor_base[0, 0, 0]
    first = base // (COLS - 1) * COLS + base % (COLS - 1)
    w = weights[0, 0, 0]
    cells = jnp.arange(CELLS, dtype=jnp.int32)[None, :]
    corner = sum(
        jnp.where(cells == (first + offset)[:, None], w[k][:, None], 0.0)
        for k, offset in enumerate((0, 1, COLS, COLS + 1))
    )
    angle = frame_angle[0, 0, 0]
    angle = jnp.broadcast_to(jnp.stack([jnp.cos(angle), jnp.sin(angle)])[:, :, None], (2, SLOTS, SHELLS))

    receiver = destination[0, 0, 0]
    slot = jnp.arange(SLOTS, dtype=jnp.int32)
    rank = jnp.sum(
        ((receiver[:, None] == receiver[None, :]) & (slot[None, :] < slot[:, None])).astype(jnp.int32), axis=1
    )
    to_row, to_col = receiver // N_PHI, receiver % N_PHI
    at_end = (to_row == 0) | (to_row == N_THETA - 1)
    mate = other * DEVS + to_row * N_PHI + jnp.where(to_col % 2 == 0, to_col + 1, to_col - 1)
    relay = patch * DEVS + to_row * N_PHI + jnp.where(ti < N_THETA // 2, to_col, (to_col + 2) % N_PHI)
    place = jnp.where(rank == 0, other * DEVS + receiver, jnp.where(at_end, relay, mate))

    def exchange(x):
        moved = lax.all_to_all(x, EVERYONE, 0, 0, tiled=True)
        direct = lax.dynamic_slice_in_dim(moved, other * DEVS, DEVS, 0)
        relayed = lax.dynamic_slice_in_dim(moved, patch * DEVS, DEVS, 0)
        from_mate = lax.ppermute(direct, "phi", [(0, 1), (1, 0), (2, 3), (3, 2)])
        early = lax.ppermute(relayed[: DEVS // 2], "patch", [(0, 1), (1, 0)])
        across = [(a * N_PHI + p, (1 - a) * N_PHI + (p + 2) % N_PHI) for a in range(2) for p in range(N_PHI)]
        late = lax.ppermute(relayed[DEVS // 2 :], ("patch", "phi"), across)
        return direct, from_mate, early, late

    position = jnp.arange(2 * DEVS, dtype=jnp.int32)
    target = target_cell[0, 0, 0]
    sent = jnp.sum(jnp.where(position[:, None] == place[None, :], target[None, :] + 1, 0), axis=1) - 1
    sent = jnp.broadcast_to(sent[:, None, None], (2 * DEVS, 1, SHELLS))
    sent, _ = lax.optimization_barrier((sent, (before, after)))
    direct, from_mate, early, late = [x[:, 0, 0] for x in exchange(sent)]
    ids = jnp.concatenate([direct, jnp.where(edge[0] + edge[1] > 0, jnp.concatenate([early, late]), from_mate)])
    ids = jnp.where(jnp.sum(edge) > 0, ids, -1)
    picked = ids[None, :] == jnp.arange(CELLS, dtype=jnp.int32)[:, None]
    pick = picked.astype(jnp.bfloat16)
    count = jnp.sum(picked.astype(jnp.float32), axis=1)
    mean = jnp.where(count > 0.0, 1.0 / jnp.maximum(count, 1.0), 0.0)
    mean = jnp.broadcast_to(mean[:, None], (CELLS, SHELLS))

    tail = (edge, row_const, phi_const, inv_r, corner, angle, place)
    top, bottom, send = run_step(False, (top, bottom, above, below, before, after, *tail))
    above, below = shift(bottom, "theta", N_THETA, 1), shift(top, "theta", N_THETA, -1)
    top, bottom, west, east, head, foot = run_merge(False, top, bottom, *exchange(send), pick, mean, edge)
    fix_above, fix_below = shift(foot, "theta", N_THETA, 1), shift(head, "theta", N_THETA, -1)
    before, after = shift(east, "phi", N_PHI, 1), shift(west, "phi", N_PHI, -1)
    top, bottom, send = run_step(
        True, (own, fix_above, fix_below, top, bottom, above, below, before, after, *tail)
    )
    (result,) = run_merge(True, top, bottom, *exchange(send), pick, mean, edge)
    return result[None]


def solution(mesh):
    placed = (
        P("patch", None, "theta", "phi", None),
        P("patch", "theta", "phi", None),
        P("patch", "theta", "phi", None, None),
        P("patch", "theta", "phi", None),
        P("patch", "theta", "phi", None),
        P("patch", "theta", "phi", None),
    )
    return jax.shard_map(
        local,
        mesh=mesh,
        in_specs=placed,
        out_specs=P("patch", None, "theta", "phi", None),
        check_vma=False,
    )
```

```python
import math

import jax
import jax.numpy as jnp
from jax import lax
from jax.experimental import pallas as pl
from jax.experimental.pallas import tpu as pltpu
from jax.sharding import PartitionSpec as P

margin = 0.03
inner_radius = 0.35
outer_radius = 1.0
gamma_ratio = 5.0 / 3.0
gravity = 1.0
rotation = 2.0
time_step = 0.002

ROWS, COLS, SHELLS, FIELDS, SLOTS = 4, 128, 128, 8, 96
HALF = ROWS // 2
CELLS = ROWS * COLS
N_THETA, N_PHI = 32, 4
DEVS = N_THETA * N_PHI
PAD = 8
EXT = COLS + 2 * PAD
THETA_STEP = (0.5 * math.pi + 2.0 * margin) / (ROWS * N_THETA)
PHI_STEP = (1.5 * math.pi + 2.0 * margin) / (COLS * N_PHI)
RADIAL_STEP = (outer_radius - inner_radius) / SHELLS
VMEM = pl.BlockSpec(memory_space=pltpu.VMEM)
SMEM = pl.BlockSpec(memory_space=pltpu.SMEM)
ANY = pl.BlockSpec(memory_space=pl.ANY)
EVERYONE = ("patch", "theta", "phi")


def struct(*shape):
    return jax.ShapeDtypeStruct(shape, jnp.float32)


HALF_BLOCK = (FIELDS, HALF, COLS, SHELLS)
RIM = (FIELDS, 8, SHELLS)
PARCEL = 2 * N_THETA + 4
CHUNK = 8


def params(mib):
    return pltpu.CompilerParams(vmem_limit_bytes=mib * 1024 * 1024)


def store_rims(top, bottom, west, east):
    for f in range(FIELDS):
        for i in range(ROWS):
            ref = (top, bottom)[i // HALF]
            west[f, 2 * i : 2 * i + 2, :] = ref[f, i % HALF, :2, :]
            east[f, 2 * i : 2 * i + 2, :] = ref[f, i % HALF, COLS - 2 :, :]


def split_kernel(fields, top, bottom, west, east, sems):
    copies = [
        pltpu.make_async_copy(fields.at[:, :HALF], top, sems.at[0]),
        pltpu.make_async_copy(fields.at[:, HALF:], bottom, sems.at[1]),
    ]
    for copy in copies:
        copy.start()
    for copy in copies:
        copy.wait()
    store_rims(top, bottom, west, east)


def run_split(fields):
    return pl.pallas_call(
        split_kernel,
        out_shape=(struct(*HALF_BLOCK), struct(*HALF_BLOCK), struct(*RIM), struct(*RIM)),
        in_specs=[ANY],
        out_specs=(VMEM,) * 4,
        scratch_shapes=[pltpu.SemaphoreType.DMA((2,))],
        compiler_params=params(16),
    )(fields)


def diff(far_low, near_low, near_high, far_high):
    return (far_low - far_high) + 8.0 * (near_high - near_low)


def step_kernel(second, *refs):
    if second:
        fix_above, fix_below, top, bottom, *refs = refs
    (
        fields, above, below, before, after, edge, row_const, phi_const, inv_r_ref, corner, angle, place,
        new_top, new_bottom, near_send, far_send, ext, donor, send, base, sems,
    ) = refs
    inside = pl.ds(PAD, COLS)
    parts = [(above, 0, HALF), (below, ROWS + 2, HALF)]
    parts += [(top, 2, HALF), (bottom, 4, HALF)] if second else [(fields, 2, ROWS)]
    copies = [
        pltpu.make_async_copy(ref, ext.at[:, start : start + rows, inside], sems.at[n])
        for n, (ref, start, rows) in enumerate(parts)
    ]
    if second:
        copies.append(pltpu.make_async_copy(fields, base, sems.at[4]))
    for copy in copies:
        copy.start()
    send[...] = jnp.zeros_like(send)
    west_edge, east_edge = edge[2] > 0, edge[3] > 0
    for f in range(FIELDS):
        for i in range(ROWS):
            pair = slice(2 * i, 2 * i + 2)
            ext[f, 2 + i, PAD - 2 : PAD, :] = jnp.where(west_edge, 0.0, before[f, pair, :])
            ext[f, 2 + i, PAD + COLS : PAD + COLS + 2, :] = jnp.where(east_edge, 0.0, after[f, pair, :])
    for copy in copies:
        copy.wait()
    if second:
        for f in range(FIELDS):
            for i in range(HALF):
                for start, ref in ((0, fix_above), (6, fix_below)):
                    ext[f, start + i, PAD : PAD + 2, :] = ref[f, 4 * i : 4 * i + 2, :]
                    ext[f, start + i, PAD + COLS - 2 : PAD + COLS, :] = ref[f, 4 * i + 2 : 4 * i + 4, :]

    @pl.when(edge[0] > 0)
    def _():
        ext[:, 0:HALF] = jnp.zeros((FIELDS, HALF, EXT, SHELLS), jnp.float32)

    @pl.when(edge[1] > 0)
    def _():
        ext[:, 6 : 6 + HALF] = jnp.zeros((FIELDS, HALF, EXT, SHELLS), jnp.float32)

    lane = lax.broadcasted_iota(jnp.int32, (8, SHELLS), 1)
    first, second_lane = lane < 1, lane < 2
    last, before_last = lane > SHELLS - 2, lane > SHELLS - 3
    inv_r = inv_r_ref[...]
    k_r = 1.0 / (12.0 * RADIAL_STEP)
    g_t = inv_r * (1.0 / (12.0 * THETA_STEP))

    def d_r(x):
        near_low = jnp.where(first, x, pltpu.roll(x, 1, 1))
        far_low = jnp.where(second_lane, near_low, pltpu.roll(x, 2, 1))
        near_high = jnp.where(last, x, pltpu.roll(x, SHELLS - 1, 1))
        far_high = jnp.where(before_last, near_high, pltpu.roll(x, SHELLS - 2, 1))
        return diff(far_low, near_low, near_high, far_high) * k_r

    for i in range(ROWS):
        sine, cosine, cot, inv_sine = [row_const[i, k] for k in range(4)]
        omega_y, omega_z = row_const[i, 4], row_const[i, 5]
        g_p = inv_r * (inv_sine * (1.0 / (12.0 * PHI_STEP)))
        cot_r = inv_r * cot
        out = (new_top, new_bottom)[i // HALF]

        def tile(j, carry):
            start = pl.multiple_of(j * 8, 8)
            rows = pl.ds(start, 8)
            padded = pl.ds(pl.multiple_of(start + PAD, 8), 8)
            q, ur, ut, up, h, br, bt, bp = [ext[f, 2 + i, padded, :] for f in range(FIELDS)]
            near = [[ext[f, 2 + i + d, padded, :] for f in range(FIELDS)] for d in (-2, -1, 1, 2)]
            tq, tur, tut, tup, th, tbr, _, tbp = [
                diff(*[n[f] for n in near]) * g_t if f != 6 else None for f in range(FIELDS)
            ]
            t_er = diff(*[n[2] * n[7] - n[3] * n[6] for n in near]) * g_t
            t_ep = diff(*[n[1] * n[6] - n[2] * n[5] for n in near]) * g_t
            near = [[ext[f, 2 + i, pl.ds(start + (PAD + d), 8), :] for f in range(FIELDS)] for d in (-2, -1, 1, 2)]
            pq, pur, put, pup, ph, pbr, pbt, _ = [
                diff(*[n[f] for n in near]) * g_p if f != 7 else None for f in range(FIELDS)
            ]
            p_er = diff(*[n[2] * n[7] - n[3] * n[6] for n in near]) * g_p
            p_et = diff(*[n[3] * n[5] - n[1] * n[7] for n in near]) * g_p
            er = ut * bp - up * bt
            et = up * br - ur * bp
            ep = ur * bt - ut * br
            rq, rur, rut, rup, rh, rbt, rbp, r_et, r_ep = [d_r(x) for x in (q, ur, ut, up, h, bt, bp, et, ep)]

            div = rur + 2.0 * ur * inv_r + tut + cot_r * ut + pup
            cur_r = tbp + cot_r * bp - pbt
            cur_t = pbr - rbp - bp * inv_r
            cur_p = rbt + bt * inv_r - tbr
            sin_phi = phi_const[0, rows, :]
            cos_phi = phi_const[1, rows, :]
            w_r = (omega_y * sine) * sin_phi + omega_z * cosine
            w_t = (omega_y * cosine) * sin_phi - omega_z * sine
            w_p = omega_y * cos_phi
            inv_rho = jnp.exp(-q)
            temper = jnp.exp(h - q)

            def adv(gr, gt, gp):
                return ur * gr + ut * gt + up * gp

            rates = [
                -adv(rq, tq, pq) - div,
                -adv(rur, tur, pur)
                + (ut * ut + up * up) * inv_r
                - temper * rh
                + inv_rho * (cur_t * bp - cur_p * bt)
                - 2.0 * (w_t * up - w_p * ut)
                - gravity * inv_r * inv_r,
                -adv(rut, tut, put)
                - (ur * ut * inv_r - cot_r * (up * up))
                - temper * th
                + inv_rho * (cur_p * br - cur_r * bp)
                - 2.0 * (w_p * ur - w_r * up),
                -adv(rup, tup, pup)
                - (ur * up * inv_r + cot_r * (ut * up))
                - temper * ph
                + inv_rho * (cur_r * bt - cur_t * br)
                - 2.0 * (w_r * ut - w_t * ur),
                -adv(rh, th, ph) - gamma_ratio * div,
                t_ep + cot_r * ep - p_et,
                p_er - r_ep - ep * inv_r,
                r_et + et * inv_r - t_er,
            ]
            centre = [q, ur, ut, up, h, br, bt, bp]
            for f in range(FIELDS):
                if second:
                    new = 0.5 * (base[f, i, rows, :] + centre[f] + time_step * rates[f])
                else:
                    new = centre[f] + time_step * rates[f]
                out[f, i % HALF, rows, :] = new
            return carry

        lax.fori_loop(0, COLS // 8, tile, 0, unroll=4)

    def product(f):
        total = None
        for n, ref in enumerate((new_top, new_bottom)):
            part = jnp.dot(
                corner[:, n * HALF * COLS : (n + 1) * HALF * COLS],
                ref[f].reshape(HALF * COLS, SHELLS),
                precision=lax.Precision.HIGHEST,
                preferred_element_type=jnp.float32,
            )
            total = part if total is None else total + part
        return total

    values = [product(f) for f in range(FIELDS)]
    c, s = angle[0], angle[1]
    for t, p in ((2, 3), (6, 7)):
        values[t], values[p] = c * values[t] - s * values[p], s * values[t] + c * values[p]
    donor[...] = jnp.swapaxes(jnp.stack(values), 0, 1)

    for m in range(0, SLOTS, 16):
        spots = [place[m + k] for k in range(16)]
        columns = [donor[m + k] for k in range(16)]
        for spot, column in zip(spots, columns):
            send[spot] = column
    near_send[...] = send[:PARCEL]
    far_send[...] = send[PARCEL:]


def run_step(second, args):
    return pl.pallas_call(
        lambda *refs: step_kernel(second, *refs),
        out_shape=(struct(*HALF_BLOCK),) * 2 + (struct(PARCEL, FIELDS, SHELLS),) * 2,
        in_specs=[VMEM] * (4 if second else 0) + [ANY] + [VMEM] * 4 + [SMEM] * 2 + [VMEM] * 4 + [SMEM],
        out_specs=(VMEM,) * 4,
        scratch_shapes=[
            pltpu.VMEM((FIELDS, ROWS + 4, EXT, SHELLS), jnp.float32),
            pltpu.VMEM((SLOTS, FIELDS, SHELLS), jnp.float32),
            pltpu.VMEM((2 * PARCEL, FIELDS, SHELLS), jnp.float32),
            pltpu.VMEM((FIELDS, ROWS if second else 1, COLS, SHELLS), jnp.float32),
            pltpu.SemaphoreType.DMA((5,)),
        ],
        compiler_params=params(24),
    )(*args)


def sort_kernel(near, far, mate_near, mate_far, core, chunks):
    for n, ref in enumerate((near, far, mate_near, mate_far)):
        for k in range(2):
            own = 2 * core[0] + k
            chunks[0, 2 * n + k] = ref[own]
            chunks[N_THETA - 1, 2 * n + k] = ref[PARCEL - 4 + own]
            for row in range(1, N_THETA - 1):
                chunks[row, 2 * n + k] = ref[2 + 2 * row + k]


def run_sort(*args):
    return pl.pallas_call(
        sort_kernel,
        out_shape=struct(N_THETA, CHUNK, FIELDS, SHELLS),
        in_specs=[VMEM] * 4 + [SMEM],
        out_specs=VMEM,
        compiler_params=params(8),
    )(*args)


def merge_kernel(last, top, bottom, moved, pick, mean, *refs):
    if last:
        merged, gathered = refs
    else:
        new_top, new_bottom, west, east, head, foot, gathered = refs
    gathered[...] = jnp.swapaxes(moved[...], 0, 1)
    weight = mean[...]
    for f in range(FIELDS):
        v = gathered[f]
        high = v.astype(jnp.bfloat16)
        rest = v - high.astype(jnp.float32)
        middle = rest.astype(jnp.bfloat16)
        low = (rest - middle.astype(jnp.float32)).astype(jnp.bfloat16)
        total = sum(jnp.dot(pick[...], x, preferred_element_type=jnp.float32) for x in (low, middle, high))
        for n, ref in enumerate((top, bottom)):
            part = slice(n * HALF * COLS, (n + 1) * HALF * COLS)
            kept = ref[f].reshape(HALF * COLS, SHELLS)
            result = jnp.where(weight[part] > 0.0, total[part] * weight[part], kept).reshape(HALF, COLS, SHELLS)
            if last:
                merged[f, n * HALF : (n + 1) * HALF] = result
            else:
                (new_top, new_bottom)[n][f] = result
    if not last:
        store_rims(new_top, new_bottom, west, east)
        for f in range(FIELDS):
            for i in range(HALF):
                for ref, fix in ((new_top, head), (new_bottom, foot)):
                    fix[f, 4 * i : 4 * i + 2, :] = ref[f, i, :2, :]
                    fix[f, 4 * i + 2 : 4 * i + 4, :] = ref[f, i, COLS - 2 :, :]


def run_merge(last, *args):
    if last:
        shapes = (struct(FIELDS, ROWS, COLS, SHELLS),)
    else:
        shapes = (struct(*HALF_BLOCK),) * 2 + (struct(*RIM),) * 4
    return pl.pallas_call(
        lambda *refs: merge_kernel(last, *refs),
        out_shape=shapes,
        in_specs=[VMEM] * 5,
        out_specs=(VMEM,) * len(shapes),
        scratch_shapes=[pltpu.VMEM((FIELDS, N_THETA * CHUNK, SHELLS), jnp.float32)],
        compiler_params=params(16),
    )(*args)


def shift(x, axis, size, by):
    return lax.ppermute(x, axis, [(i, (i + by) % size) for i in range(size)])


def local(fields, donor_base, weights, frame_angle, destination, target_cell):
    own = fields[0]
    patch, ti, pi = [lax.axis_index(axis) for axis in EVERYONE]

    top, bottom, west, east = run_split(own)
    above, below = shift(bottom, "theta", N_THETA, 1), shift(top, "theta", N_THETA, -1)
    before, after = shift(east, "phi", N_PHI, 1), shift(west, "phi", N_PHI, -1)
    edge = jnp.stack([ti == 0, ti == N_THETA - 1, pi == 0, pi == N_PHI - 1]).astype(jnp.int32)

    row_index = ti * ROWS + jnp.arange(ROWS, dtype=jnp.int32)
    theta = 0.25 * math.pi - margin + (row_index.astype(jnp.float32) + 0.5) * THETA_STEP
    col_index = pi * COLS + jnp.arange(COLS, dtype=jnp.int32)
    phi = -0.75 * math.pi - margin + (col_index.astype(jnp.float32) + 0.5) * PHI_STEP
    flag = patch.astype(jnp.float32)
    sine, cosine = jnp.sin(theta), jnp.cos(theta)
    ones = jnp.ones_like(sine)
    row_const = jnp.stack(
        [sine, cosine, cosine / sine, 1.0 / sine, ones * (rotation * flag), ones * (rotation * (1.0 - flag))], axis=1
    )
    phi_const = jnp.broadcast_to(jnp.stack([jnp.sin(phi), jnp.cos(phi)])[:, :, None], (2, COLS, SHELLS))
    radius = inner_radius + RADIAL_STEP * (jnp.arange(SHELLS, dtype=jnp.int32).astype(jnp.float32) + 0.5)
    inv_r = jnp.broadcast_to((1.0 / radius)[None, :], (8, SHELLS))

    base = donor_base[0, 0, 0]
    first = base // (COLS - 1) * COLS + base % (COLS - 1)
    w = weights[0, 0, 0]
    cells = jnp.arange(CELLS, dtype=jnp.int32)[None, :]
    corner = sum(
        jnp.where(cells == (first + offset)[:, None], w[k][:, None], 0.0)
        for k, offset in enumerate((0, 1, COLS, COLS + 1))
    )
    angle = frame_angle[0, 0, 0]
    angle = jnp.broadcast_to(jnp.stack([jnp.cos(angle), jnp.sin(angle)])[:, :, None], (2, SLOTS, SHELLS))

    receiver = destination[0, 0, 0]
    slot = jnp.arange(SLOTS, dtype=jnp.int32)
    rank = jnp.sum(
        ((receiver[:, None] == receiver[None, :]) & (slot[None, :] < slot[:, None])).astype(jnp.int32), axis=1
    )
    to_row, to_col = receiver // N_PHI, receiver % N_PHI
    end_spot = 2 * (to_col % 2) + rank
    spot = jnp.where(
        to_row == 0, end_spot, jnp.where(to_row == N_THETA - 1, PARCEL - 4 + end_spot, 2 + 2 * to_row + rank)
    )
    place = jnp.where(to_col // 2 == pi // 2, spot, PARCEL + spot)
    core = (pi % 2).astype(jnp.int32).reshape(1)

    def across(x, by):
        pairs = [(a * N_PHI + p, (1 - a) * N_PHI + (p + by) % N_PHI) for a in range(2) for p in range(N_PHI)]
        return lax.ppermute(x, ("patch", "phi"), pairs)

    def gather_pair(near, far):
        near, far = across(near, 0), across(far, 2)
        swap = [(0, 1), (1, 0), (2, 3), (3, 2)]
        return near, far, lax.ppermute(near, "phi", swap), lax.ppermute(far, "phi", swap)

    def exchange(near, far):
        chunks = run_sort(*gather_pair(near, far), core)
        chunks = chunks.reshape(N_THETA, CHUNK * FIELDS, SHELLS)
        moved = lax.all_to_all(chunks, "theta", 0, 0, tiled=True)
        return moved.reshape(N_THETA * CHUNK, FIELDS, SHELLS)

    def exchange_ids(sent):
        lanes = [jnp.pad(sent[n * PARCEL : (n + 1) * PARCEL], (0, SHELLS - PARCEL))[None] for n in range(2)]
        parts = jnp.concatenate(gather_pair(*lanes))
        inside = parts[:, 4 : PARCEL - 4].reshape(4, N_THETA - 2, 2)
        first = lax.dynamic_slice_in_dim(parts, 2 * core[0], 2, 1)[:, None]
        final = lax.dynamic_slice_in_dim(parts, PARCEL - 4 + 2 * core[0], 2, 1)[:, None]
        chunks = jnp.concatenate([first, inside, final], axis=1).swapaxes(0, 1).reshape(N_THETA, 1, CHUNK)
        chunks = jnp.pad(chunks, ((0, 0), (0, 0), (0, SHELLS - CHUNK)))
        moved = lax.all_to_all(chunks, "theta", 0, 0, tiled=True)
        return moved[:, 0, :CHUNK].reshape(N_THETA * CHUNK)

    position = jnp.arange(2 * PARCEL, dtype=jnp.int32)
    target = target_cell[0, 0, 0]
    sent = jnp.sum(jnp.where(position[:, None] == place[None, :], target[None, :] + 1, 0), axis=1) - 1
    sent, _ = lax.optimization_barrier((sent, (before, after)))
    ids = jnp.where(jnp.sum(edge) > 0, exchange_ids(sent), -1)
    picked = ids[None, :] == jnp.arange(CELLS, dtype=jnp.int32)[:, None]
    pick = picked.astype(jnp.bfloat16)
    count = jnp.sum(picked.astype(jnp.float32), axis=1)
    mean = jnp.where(count > 0.0, 1.0 / jnp.maximum(count, 1.0), 0.0)
    mean = jnp.broadcast_to(mean[:, None], (CELLS, SHELLS))

    tail = (own, above, below, before, after, edge, row_const, phi_const, inv_r, corner, angle, place)
    top, bottom, near, far = run_step(False, tail)
    above, below = shift(bottom, "theta", N_THETA, 1), shift(top, "theta", N_THETA, -1)
    top, bottom, west, east, head, foot = run_merge(False, top, bottom, exchange(near, far), pick, mean)
    fixes = shift(foot, "theta", N_THETA, 1), shift(head, "theta", N_THETA, -1)
    before, after = shift(east, "phi", N_PHI, 1), shift(west, "phi", N_PHI, -1)
    tail = (own, above, below, before, after, *tail[5:])
    top, bottom, near, far = run_step(True, (*fixes, top, bottom, *tail))
    (result,) = run_merge(True, top, bottom, exchange(near, far), pick, mean)
    return result[None]


def solution(mesh):
    placed = (
        P("patch", None, "theta", "phi", None),
        P("patch", "theta", "phi", None),
        P("patch", "theta", "phi", None, None),
        P("patch", "theta", "phi", None),
        P("patch", "theta", "phi", None),
        P("patch", "theta", "phi", None),
    )
    return jax.shard_map(
        local,
        mesh=mesh,
        in_specs=placed,
        out_specs=P("patch", None, "theta", "phi", None),
        check_vma=False,
    )
```

```python
import math

import jax
import jax.numpy as jnp
from jax import lax
from jax.experimental import pallas as pl
from jax.experimental.pallas import tpu as pltpu
from jax.sharding import PartitionSpec as P

margin = 0.03
inner_radius = 0.35
outer_radius = 1.0
gamma_ratio = 5.0 / 3.0
gravity = 1.0
rotation = 2.0
time_step = 0.002

ROWS, COLS, SHELLS, FIELDS, SLOTS = 4, 128, 128, 8, 96
HALF = ROWS // 2
CELLS = ROWS * COLS
N_THETA, N_PHI = 32, 4
DEVS = N_THETA * N_PHI
PAD = 8
EXT = COLS + 2 * PAD
THETA_STEP = (0.5 * math.pi + 2.0 * margin) / (ROWS * N_THETA)
PHI_STEP = (1.5 * math.pi + 2.0 * margin) / (COLS * N_PHI)
RADIAL_STEP = (outer_radius - inner_radius) / SHELLS
VMEM = pl.BlockSpec(memory_space=pltpu.VMEM)
SMEM = pl.BlockSpec(memory_space=pltpu.SMEM)
ANY = pl.BlockSpec(memory_space=pl.ANY)
EVERYONE = ("patch", "theta", "phi")


def struct(*shape):
    return jax.ShapeDtypeStruct(shape, jnp.float32)


BLOCK = (FIELDS, ROWS, COLS, SHELLS)
HALF_BLOCK = (FIELDS, HALF, COLS, SHELLS)
QUARTER = (FIELDS, HALF, COLS // 2, SHELLS)
RIM = (FIELDS, 8, SHELLS)
PARCEL = 2 * N_THETA + 4
CHUNK = 8


def params(mib):
    return pltpu.CompilerParams(vmem_limit_bytes=mib * 1024 * 1024)


def store_rims(block, west, east, width):
    for f in range(FIELDS):
        for i in range(ROWS):
            west[f, 2 * i : 2 * i + 2, :] = block[f, i, :2, :]
            east[f, 2 * i : 2 * i + 2, :] = block[f, i, width - 2 : width, :]


def split_kernel(fields, top, bottom, west, east, rims, sems):
    copies = [
        pltpu.make_async_copy(fields.at[:, :, :8], rims.at[:, :, :8], sems.at[0]),
        pltpu.make_async_copy(fields.at[:, :, COLS - 8 :], rims.at[:, :, 8:], sems.at[1]),
        pltpu.make_async_copy(fields.at[:, :HALF], top, sems.at[2]),
        pltpu.make_async_copy(fields.at[:, HALF:], bottom, sems.at[3]),
    ]
    for copy in copies:
        copy.start()
    for copy in copies[:2]:
        copy.wait()
    store_rims(rims, west, east, 16)
    for copy in copies[2:]:
        copy.wait()


def run_split(fields):
    return pl.pallas_call(
        split_kernel,
        out_shape=(struct(*HALF_BLOCK), struct(*HALF_BLOCK), struct(*RIM), struct(*RIM)),
        in_specs=[ANY],
        out_specs=(ANY, ANY, VMEM, VMEM),
        scratch_shapes=[pltpu.VMEM((FIELDS, ROWS, 16, SHELLS), jnp.float32), pltpu.SemaphoreType.DMA((4,))],
        compiler_params=params(8),
    )(fields)


def thirds(x):
    high = x.astype(jnp.bfloat16)
    rest = x - high.astype(jnp.float32)
    middle = rest.astype(jnp.bfloat16)
    return (rest - middle.astype(jnp.float32)).astype(jnp.bfloat16), middle, high


def diff(far_low, near_low, near_high, far_high):
    return (far_low - far_high) + 8.0 * (near_high - near_low)


def step_kernel(second, *refs):
    if second:
        fix_above, fix_below, block, above_west, above_east, below_west, below_east, *refs = refs
    else:
        above, below, *refs = refs
    fields, before, after, edge, row_const, phi_const, inv_r_ref, corner, angle, place, new, *refs = refs
    if not second:
        pieces, refs = refs[:4], refs[4:]
    near_send, far_send, ext, donor, send, base, sems = refs
    west, east, inside = pl.ds(PAD, COLS // 2), pl.ds(PAD + COLS // 2, COLS // 2), pl.ds(PAD, COLS)
    high, low = slice(0, HALF), slice(ROWS + 2, ROWS + 2 + HALF)
    if second:
        parts = [(above_west, high, west), (above_east, high, east), (below_west, low, west), (below_east, low, east)]
    else:
        parts = [(above, high, inside), (below, low, inside)]
    parts.append((block if second else fields, slice(2, 2 + ROWS), inside))
    copies = [
        pltpu.make_async_copy(ref, ext.at[:, rows, cols], sems.at[n]) for n, (ref, rows, cols) in enumerate(parts)
    ]
    if second:
        copies.append(pltpu.make_async_copy(fields, base, sems.at[5]))
    for copy in copies:
        copy.start()
    send[...] = jnp.zeros_like(send)
    west_edge, east_edge = edge[2] > 0, edge[3] > 0
    for f in range(FIELDS):
        for i in range(ROWS):
            pair = slice(2 * i, 2 * i + 2)
            ext[f, 2 + i, PAD - 2 : PAD, :] = jnp.where(west_edge, 0.0, before[f, pair, :])
            ext[f, 2 + i, PAD + COLS : PAD + COLS + 2, :] = jnp.where(east_edge, 0.0, after[f, pair, :])
    for copy in copies:
        copy.wait()
    if second:
        for f in range(FIELDS):
            for i in range(HALF):
                for start, ref in ((0, fix_above), (6, fix_below)):
                    ext[f, start + i, PAD : PAD + 2, :] = ref[f, 4 * i : 4 * i + 2, :]
                    ext[f, start + i, PAD + COLS - 2 : PAD + COLS, :] = ref[f, 4 * i + 2 : 4 * i + 4, :]

    @pl.when(edge[0] > 0)
    def _():
        ext[:, 0:HALF] = jnp.zeros((FIELDS, HALF, EXT, SHELLS), jnp.float32)

    @pl.when(edge[1] > 0)
    def _():
        ext[:, 6 : 6 + HALF] = jnp.zeros((FIELDS, HALF, EXT, SHELLS), jnp.float32)

    lane = lax.broadcasted_iota(jnp.int32, (8, SHELLS), 1)
    first, second_lane = lane < 1, lane < 2
    last, before_last = lane > SHELLS - 2, lane > SHELLS - 3
    inv_r = inv_r_ref[...]
    k_r = 1.0 / (12.0 * RADIAL_STEP)
    g_t = inv_r * (1.0 / (12.0 * THETA_STEP))

    def d_r(x):
        near_low = jnp.where(first, x, pltpu.roll(x, 1, 1))
        far_low = jnp.where(second_lane, near_low, pltpu.roll(x, 2, 1))
        near_high = jnp.where(last, x, pltpu.roll(x, SHELLS - 1, 1))
        far_high = jnp.where(before_last, near_high, pltpu.roll(x, SHELLS - 2, 1))
        return diff(far_low, near_low, near_high, far_high) * k_r

    for i in range(ROWS):
        sine, cosine, cot, inv_sine = [row_const[i, k] for k in range(4)]
        omega_y, omega_z = row_const[i, 4], row_const[i, 5]
        g_p = inv_r * (inv_sine * (1.0 / (12.0 * PHI_STEP)))
        cot_r = inv_r * cot

        def tile(j, carry):
            start = pl.multiple_of(j * 8, 8)
            rows = pl.ds(start, 8)
            padded = pl.ds(pl.multiple_of(start + PAD, 8), 8)
            q, ur, ut, up, h, br, bt, bp = [ext[f, 2 + i, padded, :] for f in range(FIELDS)]
            near = [[ext[f, 2 + i + d, padded, :] for f in range(FIELDS)] for d in (-2, -1, 1, 2)]
            tq, tur, tut, tup, th, tbr, _, tbp = [
                diff(*[n[f] for n in near]) * g_t if f != 6 else None for f in range(FIELDS)
            ]
            t_er = diff(*[n[2] * n[7] - n[3] * n[6] for n in near]) * g_t
            t_ep = diff(*[n[1] * n[6] - n[2] * n[5] for n in near]) * g_t
            near = [[ext[f, 2 + i, pl.ds(start + (PAD + d), 8), :] for f in range(FIELDS)] for d in (-2, -1, 1, 2)]
            pq, pur, put, pup, ph, pbr, pbt, _ = [
                diff(*[n[f] for n in near]) * g_p if f != 7 else None for f in range(FIELDS)
            ]
            p_er = diff(*[n[2] * n[7] - n[3] * n[6] for n in near]) * g_p
            p_et = diff(*[n[3] * n[5] - n[1] * n[7] for n in near]) * g_p
            er = ut * bp - up * bt
            et = up * br - ur * bp
            ep = ur * bt - ut * br
            rq, rur, rut, rup, rh, rbt, rbp, r_et, r_ep = [d_r(x) for x in (q, ur, ut, up, h, bt, bp, et, ep)]

            div = rur + 2.0 * ur * inv_r + tut + cot_r * ut + pup
            cur_r = tbp + cot_r * bp - pbt
            cur_t = pbr - rbp - bp * inv_r
            cur_p = rbt + bt * inv_r - tbr
            sin_phi = phi_const[0, rows, :]
            cos_phi = phi_const[1, rows, :]
            w_r = (omega_y * sine) * sin_phi + omega_z * cosine
            w_t = (omega_y * cosine) * sin_phi - omega_z * sine
            w_p = omega_y * cos_phi
            inv_rho = jnp.exp(-q)
            temper = jnp.exp(h - q)

            def adv(gr, gt, gp):
                return ur * gr + ut * gt + up * gp

            rates = [
                -adv(rq, tq, pq) - div,
                -adv(rur, tur, pur)
                + (ut * ut + up * up) * inv_r
                - temper * rh
                + inv_rho * (cur_t * bp - cur_p * bt)
                - 2.0 * (w_t * up - w_p * ut)
                - gravity * inv_r * inv_r,
                -adv(rut, tut, put)
                - (ur * ut * inv_r - cot_r * (up * up))
                - temper * th
                + inv_rho * (cur_p * br - cur_r * bp)
                - 2.0 * (w_p * ur - w_r * up),
                -adv(rup, tup, pup)
                - (ur * up * inv_r + cot_r * (ut * up))
                - temper * ph
                + inv_rho * (cur_r * bt - cur_t * br)
                - 2.0 * (w_r * ut - w_t * ur),
                -adv(rh, th, ph) - gamma_ratio * div,
                t_ep + cot_r * ep - p_et,
                p_er - r_ep - ep * inv_r,
                r_et + et * inv_r - t_er,
            ]
            centre = [q, ur, ut, up, h, br, bt, bp]
            for f in range(FIELDS):
                if second:
                    value = 0.5 * (base[f, i, rows, :] + centre[f] + time_step * rates[f])
                else:
                    value = centre[f] + time_step * rates[f]
                new[f, i, rows, :] = value
            return carry

        lax.fori_loop(0, COLS // 8, tile, 0, unroll=4)

    leaving = []
    if not second:
        for n, piece in enumerate(pieces):
            part = new.at[:, pl.ds(HALF * (n // 2), HALF), pl.ds(COLS // 2 * (n % 2), COLS // 2)]
            leaving.append(pltpu.make_async_copy(part, piece, sems.at[6 + n]))
            leaving[-1].start()

    values = []
    for f in range(0, FIELDS, 2):
        pair = jnp.concatenate([new[f + n].reshape(CELLS, SHELLS) for n in range(2)], axis=1)
        both = jnp.dot(
            corner[...], pair, precision=lax.Precision.HIGHEST, preferred_element_type=jnp.float32
        )
        values += [both[:, :SHELLS], both[:, SHELLS:]]
    c, s = angle[0], angle[1]
    for t, p in ((2, 3), (6, 7)):
        values[t], values[p] = c * values[t] - s * values[p], s * values[t] + c * values[p]
    donor[...] = jnp.swapaxes(jnp.stack(values), 0, 1)

    for m in range(0, SLOTS, 16):
        spots = [place[m + k] for k in range(16)]
        columns = [donor[m + k] for k in range(16)]
        for spot, column in zip(spots, columns):
            send[spot] = column
    near_send[...] = send[:PARCEL]
    far_send[...] = send[PARCEL:]
    for copy in leaving:
        copy.wait()


def run_step(second, args):
    pieces = 0 if second else 4
    return pl.pallas_call(
        lambda *refs: step_kernel(second, *refs),
        out_shape=(struct(*BLOCK),) + (struct(*QUARTER),) * pieces + (struct(PARCEL, FIELDS, SHELLS),) * 2,
        in_specs=([VMEM] * 2 + [ANY] * 5 if second else [ANY] * 2)
        + [ANY]
        + [VMEM] * 2
        + [SMEM] * 2
        + [VMEM] * 4
        + [SMEM],
        out_specs=(VMEM,) + (ANY,) * pieces + (VMEM,) * 2,
        scratch_shapes=[
            pltpu.VMEM((FIELDS, ROWS + 4, EXT, SHELLS), jnp.float32),
            pltpu.VMEM((SLOTS, FIELDS, SHELLS), jnp.float32),
            pltpu.VMEM((2 * PARCEL, FIELDS, SHELLS), jnp.float32),
            pltpu.VMEM((FIELDS, ROWS if second else 1, COLS, SHELLS), jnp.float32),
            pltpu.SemaphoreType.DMA((10,)),
        ],
        compiler_params=params(20),
    )(*args)


def sort_kernel(near, far, mate_near, mate_far, core, chunks):
    for n, ref in enumerate((near, far, mate_near, mate_far)):
        for k in range(2):
            own = 2 * core[0] + k
            chunks[0, 2 * n + k] = ref[own]
            chunks[N_THETA - 1, 2 * n + k] = ref[PARCEL - 4 + own]
            for row in range(1, N_THETA - 1):
                chunks[row, 2 * n + k] = ref[2 + 2 * row + k]


def run_sort(*args):
    return pl.pallas_call(
        sort_kernel,
        out_shape=struct(N_THETA, CHUNK, FIELDS, SHELLS),
        in_specs=[VMEM] * 4 + [SMEM],
        out_specs=VMEM,
        compiler_params=params(8),
    )(*args)


def merge_kernel(last, block, moved, pick, mean, merged, *refs):
    kept, gathered, sem = refs[-3:]
    copy = pltpu.make_async_copy(block, kept, sem)
    copy.start()
    columns = jnp.swapaxes(moved[...], 0, 1)
    for f in range(FIELDS):
        gathered[f // 2, :, f % 2 * SHELLS : (f % 2 + 1) * SHELLS] = columns[f]
    copy.wait()
    weight = mean[...]
    for pair in range(FIELDS // 2):
        parts = thirds(gathered[pair])
        total = sum(jnp.dot(pick[...], x, preferred_element_type=jnp.float32) for x in parts)
        for n in range(2):
            f = 2 * pair + n
            average = total[:, n * SHELLS : (n + 1) * SHELLS] * weight
            result = jnp.where(weight > 0.0, average, kept[f].reshape(CELLS, SHELLS))
            merged[f] = result.reshape(ROWS, COLS, SHELLS)
    if not last:
        west, east, head, foot = refs[:4]
        store_rims(merged, west, east, COLS)
        for f in range(FIELDS):
            for i in range(HALF):
                for row, fix in ((i, head), (HALF + i, foot)):
                    fix[f, 4 * i : 4 * i + 2, :] = merged[f, row, :2, :]
                    fix[f, 4 * i + 2 : 4 * i + 4, :] = merged[f, row, COLS - 2 :, :]


def run_merge(last, *args):
    shapes = (struct(*BLOCK),) + (() if last else (struct(*RIM),) * 4)
    return pl.pallas_call(
        lambda *refs: merge_kernel(last, *refs),
        out_shape=shapes,
        in_specs=[ANY] + [VMEM] * 3,
        out_specs=(VMEM,) * len(shapes),
        scratch_shapes=[
            pltpu.VMEM(BLOCK, jnp.float32),
            pltpu.VMEM((FIELDS // 2, N_THETA * CHUNK, 2 * SHELLS), jnp.float32),
            pltpu.SemaphoreType.DMA,
        ],
        compiler_params=params(16),
    )(*args)


def shift(x, axis, size, by):
    return lax.ppermute(x, axis, [(i, (i + by) % size) for i in range(size)])


def local(fields, donor_base, weights, frame_angle, destination, target_cell):
    own = fields[0]
    patch, ti, pi = [lax.axis_index(axis) for axis in EVERYONE]

    top, bottom, west, east = run_split(own)
    above, below = shift(bottom, "theta", N_THETA, 1), shift(top, "theta", N_THETA, -1)
    before, after = shift(east, "phi", N_PHI, 1), shift(west, "phi", N_PHI, -1)
    edge = jnp.stack([ti == 0, ti == N_THETA - 1, pi == 0, pi == N_PHI - 1]).astype(jnp.int32)

    row_index = ti * ROWS + jnp.arange(ROWS, dtype=jnp.int32)
    theta = 0.25 * math.pi - margin + (row_index.astype(jnp.float32) + 0.5) * THETA_STEP
    col_index = pi * COLS + jnp.arange(COLS, dtype=jnp.int32)
    phi = -0.75 * math.pi - margin + (col_index.astype(jnp.float32) + 0.5) * PHI_STEP
    flag = patch.astype(jnp.float32)
    sine, cosine = jnp.sin(theta), jnp.cos(theta)
    ones = jnp.ones_like(sine)
    row_const = jnp.stack(
        [sine, cosine, cosine / sine, 1.0 / sine, ones * (rotation * flag), ones * (rotation * (1.0 - flag))], axis=1
    )
    phi_const = jnp.broadcast_to(jnp.stack([jnp.sin(phi), jnp.cos(phi)])[:, :, None], (2, COLS, SHELLS))
    radius = inner_radius + RADIAL_STEP * (jnp.arange(SHELLS, dtype=jnp.int32).astype(jnp.float32) + 0.5)
    inv_r = jnp.broadcast_to((1.0 / radius)[None, :], (8, SHELLS))

    base = donor_base[0, 0, 0]
    first = base // (COLS - 1) * COLS + base % (COLS - 1)
    w = weights[0, 0, 0]
    cells = jnp.arange(CELLS, dtype=jnp.int32)[None, :]
    corner = sum(
        jnp.where(cells == (first + offset)[:, None], w[k][:, None], 0.0)
        for k, offset in enumerate((0, 1, COLS, COLS + 1))
    )
    angle = frame_angle[0, 0, 0]
    angle = jnp.broadcast_to(jnp.stack([jnp.cos(angle), jnp.sin(angle)])[:, :, None], (2, SLOTS, SHELLS))

    receiver = destination[0, 0, 0]
    slot = jnp.arange(SLOTS, dtype=jnp.int32)
    rank = jnp.sum(
        ((receiver[:, None] == receiver[None, :]) & (slot[None, :] < slot[:, None])).astype(jnp.int32), axis=1
    )
    to_row, to_col = receiver // N_PHI, receiver % N_PHI
    end_spot = 2 * (to_col % 2) + rank
    spot = jnp.where(
        to_row == 0, end_spot, jnp.where(to_row == N_THETA - 1, PARCEL - 4 + end_spot, 2 + 2 * to_row + rank)
    )
    place = jnp.where(to_col // 2 == pi // 2, spot, PARCEL + spot)
    core = (pi % 2).astype(jnp.int32).reshape(1)

    def across(x, by):
        pairs = [(a * N_PHI + p, (1 - a) * N_PHI + (p + by) % N_PHI) for a in range(2) for p in range(N_PHI)]
        return lax.ppermute(x, ("patch", "phi"), pairs)

    def gather_pair(near, far):
        near, far = across(near, 0), across(far, 2)
        swap = [(0, 1), (1, 0), (2, 3), (3, 2)]
        return near, far, lax.ppermute(near, "phi", swap), lax.ppermute(far, "phi", swap)

    def exchange(near, far, *first):
        chunks = run_sort(*gather_pair(near, far), core)
        chunks, first = lax.optimization_barrier((chunks, first))
        chunks = chunks.reshape(N_THETA, CHUNK * FIELDS, SHELLS)
        moved = lax.all_to_all(chunks, "theta", 0, 0, tiled=True)
        return moved.reshape(N_THETA * CHUNK, FIELDS, SHELLS), *first

    def exchange_ids(sent):
        lanes = [jnp.pad(sent[n * PARCEL : (n + 1) * PARCEL], (0, SHELLS - PARCEL))[None] for n in range(2)]
        parts = jnp.concatenate(gather_pair(*lanes))
        inside = parts[:, 4 : PARCEL - 4].reshape(4, N_THETA - 2, 2)
        first = lax.dynamic_slice_in_dim(parts, 2 * core[0], 2, 1)[:, None]
        final = lax.dynamic_slice_in_dim(parts, PARCEL - 4 + 2 * core[0], 2, 1)[:, None]
        chunks = jnp.concatenate([first, inside, final], axis=1).swapaxes(0, 1).reshape(N_THETA, 1, CHUNK)
        chunks = jnp.pad(chunks, ((0, 0), (0, 0), (0, SHELLS - CHUNK)))
        moved = lax.all_to_all(chunks, "theta", 0, 0, tiled=True)
        return moved[:, 0, :CHUNK].reshape(N_THETA * CHUNK)

    position = jnp.arange(2 * PARCEL, dtype=jnp.int32)
    target = target_cell[0, 0, 0]
    sent = jnp.sum(jnp.where(position[:, None] == place[None, :], target[None, :] + 1, 0), axis=1) - 1
    sent, _ = lax.optimization_barrier((sent, (before, after)))
    ids = jnp.where(jnp.sum(edge) > 0, exchange_ids(sent), -1)
    picked = ids[None, :] == jnp.arange(CELLS, dtype=jnp.int32)[:, None]
    pick = picked.astype(jnp.bfloat16)
    count = jnp.sum(picked.astype(jnp.float32), axis=1)
    mean = jnp.where(count > 0.0, 1.0 / jnp.maximum(count, 1.0), 0.0)
    mean = jnp.broadcast_to(mean[:, None], (CELLS, SHELLS))

    edge, pick = lax.optimization_barrier((edge, pick))
    tail = (edge, row_const, phi_const, inv_r, corner, angle, place)
    block, *pieces, near, far = run_step(False, (above, below, own, before, after, *tail))
    above_west, above_east = [shift(x, "theta", N_THETA, 1) for x in pieces[2:]]
    below_west, below_east = [shift(x, "theta", N_THETA, -1) for x in pieces[:2]]
    moved, above_west, below_west = exchange(near, far, above_west, below_west)
    block, west, east, head, foot = run_merge(False, block, moved, pick, mean)
    fixes = shift(foot, "theta", N_THETA, 1), shift(head, "theta", N_THETA, -1)
    before, after = shift(east, "phi", N_PHI, 1), shift(west, "phi", N_PHI, -1)
    halo = (above_west, above_east, below_west, below_east)
    block, near, far = run_step(True, (*fixes, block, *halo, own, before, after, *tail))
    (result,) = run_merge(True, block, *exchange(near, far), pick, mean)
    return result[None]


def solution(mesh):
    placed = (
        P("patch", None, "theta", "phi", None),
        P("patch", "theta", "phi", None),
        P("patch", "theta", "phi", None, None),
        P("patch", "theta", "phi", None),
        P("patch", "theta", "phi", None),
        P("patch", "theta", "phi", None),
    )
    return jax.shard_map(
        local,
        mesh=mesh,
        in_specs=placed,
        out_specs=P("patch", None, "theta", "phi", None),
        check_vma=False,
    )
```

```python
import math

import jax
import jax.numpy as jnp
from jax import lax
from jax.experimental import pallas as pl
from jax.experimental.pallas import tpu as pltpu
from jax.sharding import PartitionSpec as P

margin = 0.03
inner_radius = 0.35
outer_radius = 1.0
gamma_ratio = 5.0 / 3.0
gravity = 1.0
rotation = 2.0
time_step = 0.002

ROWS, COLS, SHELLS, FIELDS, SLOTS = 4, 128, 128, 8, 96
HALF = ROWS // 2
CELLS = ROWS * COLS
N_THETA, N_PHI = 32, 4
DEVS = N_THETA * N_PHI
PAD = 8
EXT = COLS + 2 * PAD
THETA_STEP = (0.5 * math.pi + 2.0 * margin) / (ROWS * N_THETA)
PHI_STEP = (1.5 * math.pi + 2.0 * margin) / (COLS * N_PHI)
RADIAL_STEP = (outer_radius - inner_radius) / SHELLS
VMEM = pl.BlockSpec(memory_space=pltpu.VMEM)
SMEM = pl.BlockSpec(memory_space=pltpu.SMEM)
ANY = pl.BlockSpec(memory_space=pl.ANY)
EVERYONE = ("patch", "theta", "phi")


def struct(*shape):
    return jax.ShapeDtypeStruct(shape, jnp.float32)


BLOCK = (FIELDS, ROWS, COLS, SHELLS)
HALF_BLOCK = (FIELDS, HALF, COLS, SHELLS)
EARLY = 48
RIM = (FIELDS, 8, SHELLS)
PARCEL = 2 * N_THETA + 4
CHUNK = 8


def params(mib):
    return pltpu.CompilerParams(vmem_limit_bytes=mib * 1024 * 1024)


def store_rims(block, west, east, width):
    for f in range(FIELDS):
        for i in range(ROWS):
            west[f, 2 * i : 2 * i + 2, :] = block[f, i, :2, :]
            east[f, 2 * i : 2 * i + 2, :] = block[f, i, width - 2 : width, :]


def split_kernel(fields, top, bottom, west, east, rims, sems):
    copies = [
        pltpu.make_async_copy(fields.at[:, :, :8], rims.at[:, :, :8], sems.at[0]),
        pltpu.make_async_copy(fields.at[:, :, COLS - 8 :], rims.at[:, :, 8:], sems.at[1]),
        pltpu.make_async_copy(fields.at[:, :HALF], top, sems.at[2]),
        pltpu.make_async_copy(fields.at[:, HALF:], bottom, sems.at[3]),
    ]
    for copy in copies:
        copy.start()
    for copy in copies[:2]:
        copy.wait()
    store_rims(rims, west, east, 16)
    for copy in copies[2:]:
        copy.wait()


def run_split(fields):
    return pl.pallas_call(
        split_kernel,
        out_shape=(struct(*HALF_BLOCK), struct(*HALF_BLOCK), struct(*RIM), struct(*RIM)),
        in_specs=[ANY],
        out_specs=(ANY, ANY, VMEM, VMEM),
        scratch_shapes=[pltpu.VMEM((FIELDS, ROWS, 16, SHELLS), jnp.float32), pltpu.SemaphoreType.DMA((4,))],
        compiler_params=params(8),
    )(fields)


def thirds(x):
    high = x.astype(jnp.bfloat16)
    rest = x - high.astype(jnp.float32)
    middle = rest.astype(jnp.bfloat16)
    return (rest - middle.astype(jnp.float32)).astype(jnp.bfloat16), middle, high


def diff(far_low, near_low, near_high, far_high):
    return (far_low - far_high) + 8.0 * (near_high - near_low)


def step_kernel(second, *refs):
    if second:
        fix_above, fix_below, block, above_west, above_east, below_west, below_east, *refs = refs
    else:
        above, below, *refs = refs
    fields, before, after, edge, row_const, phi_const, inv_r_ref, corner, angle, place, new, *refs = refs
    if not second:
        pieces, refs = refs[:4], refs[4:]
    near_send, far_send, ext, donor, send, base, sems = refs
    west, east, inside = pl.ds(PAD, EARLY), pl.ds(PAD + EARLY, COLS - EARLY), pl.ds(PAD, COLS)
    high, low = slice(0, HALF), slice(ROWS + 2, ROWS + 2 + HALF)
    if second:
        parts = [(above_west, high, west), (above_east, high, east), (below_west, low, west), (below_east, low, east)]
    else:
        parts = [(above, high, inside), (below, low, inside)]
    parts.append((block if second else fields, slice(2, 2 + ROWS), inside))
    copies = [
        pltpu.make_async_copy(ref, ext.at[:, rows, cols], sems.at[n]) for n, (ref, rows, cols) in enumerate(parts)
    ]
    if second:
        copies.append(pltpu.make_async_copy(fields, base, sems.at[5]))
    for copy in copies:
        copy.start()
    send[...] = jnp.zeros_like(send)
    west_edge, east_edge = edge[2] > 0, edge[3] > 0
    for f in range(FIELDS):
        for i in range(ROWS):
            pair = slice(2 * i, 2 * i + 2)
            ext[f, 2 + i, PAD - 2 : PAD, :] = jnp.where(west_edge, 0.0, before[f, pair, :])
            ext[f, 2 + i, PAD + COLS : PAD + COLS + 2, :] = jnp.where(east_edge, 0.0, after[f, pair, :])
    for copy in copies:
        copy.wait()
    if second:
        for f in range(FIELDS):
            for i in range(HALF):
                for start, ref in ((0, fix_above), (6, fix_below)):
                    ext[f, start + i, PAD : PAD + 2, :] = ref[f, 4 * i : 4 * i + 2, :]
                    ext[f, start + i, PAD + COLS - 2 : PAD + COLS, :] = ref[f, 4 * i + 2 : 4 * i + 4, :]

    @pl.when(edge[0] > 0)
    def _():
        ext[:, 0:HALF] = jnp.zeros((FIELDS, HALF, EXT, SHELLS), jnp.float32)

    @pl.when(edge[1] > 0)
    def _():
        ext[:, 6 : 6 + HALF] = jnp.zeros((FIELDS, HALF, EXT, SHELLS), jnp.float32)

    lane = lax.broadcasted_iota(jnp.int32, (8, SHELLS), 1)
    first, second_lane = lane < 1, lane < 2
    last, before_last = lane > SHELLS - 2, lane > SHELLS - 3
    inv_r = inv_r_ref[...]
    k_r = 1.0 / (12.0 * RADIAL_STEP)
    g_t = inv_r * (1.0 / (12.0 * THETA_STEP))

    def d_r(x):
        near_low = jnp.where(first, x, pltpu.roll(x, 1, 1))
        far_low = jnp.where(second_lane, near_low, pltpu.roll(x, 2, 1))
        near_high = jnp.where(last, x, pltpu.roll(x, SHELLS - 1, 1))
        far_high = jnp.where(before_last, near_high, pltpu.roll(x, SHELLS - 2, 1))
        return diff(far_low, near_low, near_high, far_high) * k_r

    for i in range(ROWS):
        sine, cosine, cot, inv_sine = [row_const[i, k] for k in range(4)]
        omega_y, omega_z = row_const[i, 4], row_const[i, 5]
        g_p = inv_r * (inv_sine * (1.0 / (12.0 * PHI_STEP)))
        cot_r = inv_r * cot

        def tile(j, carry):
            start = pl.multiple_of(j * 8, 8)
            rows = pl.ds(start, 8)
            padded = pl.ds(pl.multiple_of(start + PAD, 8), 8)
            q, ur, ut, up, h, br, bt, bp = [ext[f, 2 + i, padded, :] for f in range(FIELDS)]
            near = [[ext[f, 2 + i + d, padded, :] for f in range(FIELDS)] for d in (-2, -1, 1, 2)]
            tq, tur, tut, tup, th, tbr, _, tbp = [
                diff(*[n[f] for n in near]) * g_t if f != 6 else None for f in range(FIELDS)
            ]
            t_er = diff(*[n[2] * n[7] - n[3] * n[6] for n in near]) * g_t
            t_ep = diff(*[n[1] * n[6] - n[2] * n[5] for n in near]) * g_t
            near = [[ext[f, 2 + i, pl.ds(start + (PAD + d), 8), :] for f in range(FIELDS)] for d in (-2, -1, 1, 2)]
            pq, pur, put, pup, ph, pbr, pbt, _ = [
                diff(*[n[f] for n in near]) * g_p if f != 7 else None for f in range(FIELDS)
            ]
            p_er = diff(*[n[2] * n[7] - n[3] * n[6] for n in near]) * g_p
            p_et = diff(*[n[3] * n[5] - n[1] * n[7] for n in near]) * g_p
            er = ut * bp - up * bt
            et = up * br - ur * bp
            ep = ur * bt - ut * br
            rq, rur, rut, rup, rh, rbt, rbp, r_et, r_ep = [d_r(x) for x in (q, ur, ut, up, h, bt, bp, et, ep)]

            div = rur + 2.0 * ur * inv_r + tut + cot_r * ut + pup
            cur_r = tbp + cot_r * bp - pbt
            cur_t = pbr - rbp - bp * inv_r
            cur_p = rbt + bt * inv_r - tbr
            sin_phi = phi_const[0, rows, :]
            cos_phi = phi_const[1, rows, :]
            w_r = (omega_y * sine) * sin_phi + omega_z * cosine
            w_t = (omega_y * cosine) * sin_phi - omega_z * sine
            w_p = omega_y * cos_phi
            inv_rho = jnp.exp(-q)
            temper = jnp.exp(h - q)

            def adv(gr, gt, gp):
                return ur * gr + ut * gt + up * gp

            rates = [
                -adv(rq, tq, pq) - div,
                -adv(rur, tur, pur)
                + (ut * ut + up * up) * inv_r
                - temper * rh
                + inv_rho * (cur_t * bp - cur_p * bt)
                - 2.0 * (w_t * up - w_p * ut)
                - gravity * inv_r * inv_r,
                -adv(rut, tut, put)
                - (ur * ut * inv_r - cot_r * (up * up))
                - temper * th
                + inv_rho * (cur_p * br - cur_r * bp)
                - 2.0 * (w_p * ur - w_r * up),
                -adv(rup, tup, pup)
                - (ur * up * inv_r + cot_r * (ut * up))
                - temper * ph
                + inv_rho * (cur_r * bt - cur_t * br)
                - 2.0 * (w_r * ut - w_t * ur),
                -adv(rh, th, ph) - gamma_ratio * div,
                t_ep + cot_r * ep - p_et,
                p_er - r_ep - ep * inv_r,
                r_et + et * inv_r - t_er,
            ]
            centre = [q, ur, ut, up, h, br, bt, bp]
            for f in range(FIELDS):
                if second:
                    value = 0.5 * (base[f, i, rows, :] + centre[f] + time_step * rates[f])
                else:
                    value = centre[f] + time_step * rates[f]
                new[f, i, rows, :] = value
            return carry

        lax.fori_loop(0, COLS // 8, tile, 0, unroll=4)

    leaving = []
    if not second:
        for n, piece in enumerate(pieces):
            cols = (pl.ds(0, EARLY), pl.ds(EARLY, COLS - EARLY))[n % 2]
            part = new.at[:, pl.ds(HALF * (n // 2), HALF), cols]
            leaving.append(pltpu.make_async_copy(part, piece, sems.at[6 + n]))
            leaving[-1].start()

    values = []
    for f in range(0, FIELDS, 2):
        pair = jnp.concatenate([new[f + n].reshape(CELLS, SHELLS) for n in range(2)], axis=1)
        both = jnp.dot(
            corner[...], pair, precision=lax.Precision.HIGHEST, preferred_element_type=jnp.float32
        )
        values += [both[:, :SHELLS], both[:, SHELLS:]]
    c, s = angle[0], angle[1]
    for t, p in ((2, 3), (6, 7)):
        values[t], values[p] = c * values[t] - s * values[p], s * values[t] + c * values[p]
    donor[...] = jnp.swapaxes(jnp.stack(values), 0, 1)

    for m in range(0, SLOTS, 16):
        spots = [place[m + k] for k in range(16)]
        columns = [donor[m + k] for k in range(16)]
        for spot, column in zip(spots, columns):
            send[spot] = column
    near_send[...] = send[:PARCEL]
    far_send[...] = send[PARCEL:]
    for copy in leaving:
        copy.wait()


def run_step(second, args):
    pieces = () if second else tuple(struct(FIELDS, HALF, n, SHELLS) for n in (EARLY, COLS - EARLY)) * 2
    return pl.pallas_call(
        lambda *refs: step_kernel(second, *refs),
        out_shape=(struct(*BLOCK), *pieces) + (struct(PARCEL, FIELDS, SHELLS),) * 2,
        in_specs=([VMEM] * 2 + [ANY] * 5 if second else [ANY] * 2)
        + [ANY]
        + [VMEM] * 2
        + [SMEM] * 2
        + [VMEM] * 4
        + [SMEM],
        out_specs=(VMEM,) + (ANY,) * len(pieces) + (VMEM,) * 2,
        scratch_shapes=[
            pltpu.VMEM((FIELDS, ROWS + 4, EXT, SHELLS), jnp.float32),
            pltpu.VMEM((SLOTS, FIELDS, SHELLS), jnp.float32),
            pltpu.VMEM((2 * PARCEL, FIELDS, SHELLS), jnp.float32),
            pltpu.VMEM((FIELDS, ROWS if second else 1, COLS, SHELLS), jnp.float32),
            pltpu.SemaphoreType.DMA((10,)),
        ],
        compiler_params=params(20),
    )(*args)


def sort_kernel(near, far, mate_near, mate_far, core, chunks):
    for n, ref in enumerate((near, far, mate_near, mate_far)):
        for k in range(2):
            own = 2 * core[0] + k
            chunks[0, 2 * n + k] = ref[own]
            chunks[N_THETA - 1, 2 * n + k] = ref[PARCEL - 4 + own]
            for row in range(1, N_THETA - 1):
                chunks[row, 2 * n + k] = ref[2 + 2 * row + k]


def run_sort(*args):
    return pl.pallas_call(
        sort_kernel,
        out_shape=struct(N_THETA, CHUNK, FIELDS, SHELLS),
        in_specs=[VMEM] * 4 + [SMEM],
        out_specs=VMEM,
        compiler_params=params(8),
    )(*args)


def merge_kernel(last, block, moved, pick, mean, merged, *refs):
    kept, gathered, sem = refs[-3:]
    copy = pltpu.make_async_copy(block, kept, sem)
    copy.start()
    columns = jnp.swapaxes(moved[...], 0, 1)
    for f in range(FIELDS):
        gathered[f // 2, :, f % 2 * SHELLS : (f % 2 + 1) * SHELLS] = columns[f]
    copy.wait()
    weight = mean[...]
    for pair in range(FIELDS // 2):
        parts = thirds(gathered[pair])
        total = sum(jnp.dot(pick[...], x, preferred_element_type=jnp.float32) for x in parts)
        for n in range(2):
            f = 2 * pair + n
            average = total[:, n * SHELLS : (n + 1) * SHELLS] * weight
            result = jnp.where(weight > 0.0, average, kept[f].reshape(CELLS, SHELLS))
            merged[f] = result.reshape(ROWS, COLS, SHELLS)
    if not last:
        west, east, head, foot = refs[:4]
        store_rims(merged, west, east, COLS)
        for f in range(FIELDS):
            for i in range(HALF):
                for row, fix in ((i, head), (HALF + i, foot)):
                    fix[f, 4 * i : 4 * i + 2, :] = merged[f, row, :2, :]
                    fix[f, 4 * i + 2 : 4 * i + 4, :] = merged[f, row, COLS - 2 :, :]


def run_merge(last, *args):
    shapes = (struct(*BLOCK),) + (() if last else (struct(*RIM),) * 4)
    return pl.pallas_call(
        lambda *refs: merge_kernel(last, *refs),
        out_shape=shapes,
        in_specs=[ANY] + [VMEM] * 3,
        out_specs=(VMEM,) * len(shapes),
        scratch_shapes=[
            pltpu.VMEM(BLOCK, jnp.float32),
            pltpu.VMEM((FIELDS // 2, N_THETA * CHUNK, 2 * SHELLS), jnp.float32),
            pltpu.SemaphoreType.DMA,
        ],
        compiler_params=params(16),
    )(*args)


def shift(x, axis, size, by):
    return lax.ppermute(x, axis, [(i, (i + by) % size) for i in range(size)])


def local(fields, donor_base, weights, frame_angle, destination, target_cell):
    own = fields[0]
    patch, ti, pi = [lax.axis_index(axis) for axis in EVERYONE]

    top, bottom, west, east = run_split(own)
    above, below = shift(bottom, "theta", N_THETA, 1), shift(top, "theta", N_THETA, -1)
    before, after = shift(east, "phi", N_PHI, 1), shift(west, "phi", N_PHI, -1)
    edge = jnp.stack([ti == 0, ti == N_THETA - 1, pi == 0, pi == N_PHI - 1]).astype(jnp.int32)

    row_index = ti * ROWS + jnp.arange(ROWS, dtype=jnp.int32)
    theta = 0.25 * math.pi - margin + (row_index.astype(jnp.float32) + 0.5) * THETA_STEP
    col_index = pi * COLS + jnp.arange(COLS, dtype=jnp.int32)
    phi = -0.75 * math.pi - margin + (col_index.astype(jnp.float32) + 0.5) * PHI_STEP
    flag = patch.astype(jnp.float32)
    sine, cosine = jnp.sin(theta), jnp.cos(theta)
    ones = jnp.ones_like(sine)
    row_const = jnp.stack(
        [sine, cosine, cosine / sine, 1.0 / sine, ones * (rotation * flag), ones * (rotation * (1.0 - flag))], axis=1
    )
    phi_const = jnp.broadcast_to(jnp.stack([jnp.sin(phi), jnp.cos(phi)])[:, :, None], (2, COLS, SHELLS))
    radius = inner_radius + RADIAL_STEP * (jnp.arange(SHELLS, dtype=jnp.int32).astype(jnp.float32) + 0.5)
    inv_r = jnp.broadcast_to((1.0 / radius)[None, :], (8, SHELLS))

    base = donor_base[0, 0, 0]
    first = base // (COLS - 1) * COLS + base % (COLS - 1)
    w = weights[0, 0, 0]
    cells = jnp.arange(CELLS, dtype=jnp.int32)[None, :]
    corner = sum(
        jnp.where(cells == (first + offset)[:, None], w[k][:, None], 0.0)
        for k, offset in enumerate((0, 1, COLS, COLS + 1))
    )
    angle = frame_angle[0, 0, 0]
    angle = jnp.broadcast_to(jnp.stack([jnp.cos(angle), jnp.sin(angle)])[:, :, None], (2, SLOTS, SHELLS))

    receiver = destination[0, 0, 0]
    slot = jnp.arange(SLOTS, dtype=jnp.int32)
    rank = jnp.sum(
        ((receiver[:, None] == receiver[None, :]) & (slot[None, :] < slot[:, None])).astype(jnp.int32), axis=1
    )
    to_row, to_col = receiver // N_PHI, receiver % N_PHI
    end_spot = 2 * (to_col % 2) + rank
    spot = jnp.where(
        to_row == 0, end_spot, jnp.where(to_row == N_THETA - 1, PARCEL - 4 + end_spot, 2 + 2 * to_row + rank)
    )
    place = jnp.where(to_col // 2 == pi // 2, spot, PARCEL + spot)
    core = (pi % 2).astype(jnp.int32).reshape(1)

    def across(x, by):
        pairs = [(a * N_PHI + p, (1 - a) * N_PHI + (p + by) % N_PHI) for a in range(2) for p in range(N_PHI)]
        return lax.ppermute(x, ("patch", "phi"), pairs)

    def gather_pair(near, far):
        near, far = across(near, 0), across(far, 2)
        swap = [(0, 1), (1, 0), (2, 3), (3, 2)]
        return near, far, lax.ppermute(near, "phi", swap), lax.ppermute(far, "phi", swap)

    def exchange(near, far, *first):
        chunks = run_sort(*gather_pair(near, far), core)
        chunks, first = lax.optimization_barrier((chunks, first))
        chunks = chunks.reshape(N_THETA, CHUNK * FIELDS, SHELLS)
        moved = lax.all_to_all(chunks, "theta", 0, 0, tiled=True)
        return moved.reshape(N_THETA * CHUNK, FIELDS, SHELLS), *first

    def exchange_ids(sent):
        lanes = [jnp.pad(sent[n * PARCEL : (n + 1) * PARCEL], (0, SHELLS - PARCEL))[None] for n in range(2)]
        parts = jnp.concatenate(gather_pair(*lanes))
        inside = parts[:, 4 : PARCEL - 4].reshape(4, N_THETA - 2, 2)
        first = lax.dynamic_slice_in_dim(parts, 2 * core[0], 2, 1)[:, None]
        final = lax.dynamic_slice_in_dim(parts, PARCEL - 4 + 2 * core[0], 2, 1)[:, None]
        chunks = jnp.concatenate([first, inside, final], axis=1).swapaxes(0, 1).reshape(N_THETA, 1, CHUNK)
        chunks = jnp.pad(chunks, ((0, 0), (0, 0), (0, SHELLS - CHUNK)))
        moved = lax.all_to_all(chunks, "theta", 0, 0, tiled=True)
        return moved[:, 0, :CHUNK].reshape(N_THETA * CHUNK)

    position = jnp.arange(2 * PARCEL, dtype=jnp.int32)
    target = target_cell[0, 0, 0]
    sent = jnp.sum(jnp.where(position[:, None] == place[None, :], target[None, :] + 1, 0), axis=1) - 1
    sent, _ = lax.optimization_barrier((sent, (before, after)))
    ids = jnp.where(jnp.sum(edge) > 0, exchange_ids(sent), -1)
    picked = ids[None, :] == jnp.arange(CELLS, dtype=jnp.int32)[:, None]
    pick = picked.astype(jnp.bfloat16)
    count = jnp.sum(picked.astype(jnp.float32), axis=1)
    mean = jnp.where(count > 0.0, 1.0 / jnp.maximum(count, 1.0), 0.0)
    mean = jnp.broadcast_to(mean[:, None], (CELLS, SHELLS))

    edge, pick = lax.optimization_barrier((edge, pick))
    tail = (edge, row_const, phi_const, inv_r, corner, angle, place)
    block, *pieces, near, far = run_step(False, (above, below, own, before, after, *tail))
    above_west, above_east = [shift(x, "theta", N_THETA, 1) for x in pieces[2:]]
    below_west, below_east = [shift(x, "theta", N_THETA, -1) for x in pieces[:2]]
    moved, above_west, below_west = exchange(near, far, above_west, below_west)
    block, west, east, head, foot = run_merge(False, block, moved, pick, mean)
    fixes = shift(foot, "theta", N_THETA, 1), shift(head, "theta", N_THETA, -1)
    before, after = shift(east, "phi", N_PHI, 1), shift(west, "phi", N_PHI, -1)
    halo = (above_west, above_east, below_west, below_east)
    block, near, far = run_step(True, (*fixes, block, *halo, own, before, after, *tail))
    (result,) = run_merge(True, block, *exchange(near, far), pick, mean)
    return result[None]


def solution(mesh):
    placed = (
        P("patch", None, "theta", "phi", None),
        P("patch", "theta", "phi", None),
        P("patch", "theta", "phi", None, None),
        P("patch", "theta", "phi", None),
        P("patch", "theta", "phi", None),
        P("patch", "theta", "phi", None),
    )
    return jax.shard_map(
        local,
        mesh=mesh,
        in_specs=placed,
        out_specs=P("patch", None, "theta", "phi", None),
        check_vma=False,
    )
```

```python
import math

import jax
import jax.numpy as jnp
from jax import lax
from jax.experimental import pallas as pl
from jax.experimental.pallas import tpu as pltpu
from jax.sharding import PartitionSpec as P

margin = 0.03
inner_radius = 0.35
outer_radius = 1.0
gamma_ratio = 5.0 / 3.0
gravity = 1.0
rotation = 2.0
time_step = 0.002

ROWS, COLS, SHELLS, FIELDS, SLOTS = 4, 128, 128, 8, 96
HALF = ROWS // 2
CELLS = ROWS * COLS
N_THETA, N_PHI = 32, 4
DEVS = N_THETA * N_PHI
PAD = 8
EXT = COLS + 2 * PAD
THETA_STEP = (0.5 * math.pi + 2.0 * margin) / (ROWS * N_THETA)
PHI_STEP = (1.5 * math.pi + 2.0 * margin) / (COLS * N_PHI)
RADIAL_STEP = (outer_radius - inner_radius) / SHELLS
VMEM = pl.BlockSpec(memory_space=pltpu.VMEM)
SMEM = pl.BlockSpec(memory_space=pltpu.SMEM)
ANY = pl.BlockSpec(memory_space=pl.ANY)
EVERYONE = ("patch", "theta", "phi")


def struct(*shape):
    return jax.ShapeDtypeStruct(shape, jnp.float32)


BLOCK = (FIELDS, ROWS, COLS, SHELLS)
HALF_BLOCK = (FIELDS, HALF, COLS, SHELLS)
EARLY = 48
RIM = (FIELDS, 8, SHELLS)
PARCEL = 2 * N_THETA + 4
CHUNK = 8


def params(mib):
    return pltpu.CompilerParams(vmem_limit_bytes=mib * 1024 * 1024)


def store_rims(block, west, east, width):
    for f in range(FIELDS):
        for i in range(ROWS):
            west[f, 2 * i : 2 * i + 2, :] = block[f, i, :2, :]
            east[f, 2 * i : 2 * i + 2, :] = block[f, i, width - 2 : width, :]


def split_kernel(fields, top, bottom, west, east, rims, sems):
    copies = [
        pltpu.make_async_copy(fields.at[:, :, :8], rims.at[:, :, :8], sems.at[0]),
        pltpu.make_async_copy(fields.at[:, :, COLS - 8 :], rims.at[:, :, 8:], sems.at[1]),
        pltpu.make_async_copy(fields.at[:, :HALF], top, sems.at[2]),
        pltpu.make_async_copy(fields.at[:, HALF:], bottom, sems.at[3]),
    ]
    for copy in copies:
        copy.start()
    for copy in copies[:2]:
        copy.wait()
    store_rims(rims, west, east, 16)
    for copy in copies[2:]:
        copy.wait()


def run_split(fields):
    return pl.pallas_call(
        split_kernel,
        out_shape=(struct(*HALF_BLOCK), struct(*HALF_BLOCK), struct(*RIM), struct(*RIM)),
        in_specs=[ANY],
        out_specs=(ANY, ANY, VMEM, VMEM),
        scratch_shapes=[pltpu.VMEM((FIELDS, ROWS, 16, SHELLS), jnp.float32), pltpu.SemaphoreType.DMA((4,))],
        compiler_params=params(8),
    )(fields)


def thirds(x):
    high = x.astype(jnp.bfloat16)
    rest = x - high.astype(jnp.float32)
    middle = rest.astype(jnp.bfloat16)
    return (rest - middle.astype(jnp.float32)).astype(jnp.bfloat16), middle, high


def diff(far_low, near_low, near_high, far_high):
    return (far_low - far_high) + 8.0 * (near_high - near_low)


def step_kernel(second, *refs):
    if second:
        fix_above, fix_below, block, above_west, above_east, below_west, below_east, *refs = refs
    else:
        above, below, *refs = refs
    fields, before, after, edge, row_const, phi_const, inv_r_ref, corner, angle, place, new, *refs = refs
    if not second:
        pieces, refs = refs[:4], refs[4:]
    near_send, far_send, ext, donor, send, base, sems = refs
    west, east, inside = pl.ds(PAD, EARLY), pl.ds(PAD + EARLY, COLS - EARLY), pl.ds(PAD, COLS)
    high, low = slice(0, HALF), slice(ROWS + 2, ROWS + 2 + HALF)
    if second:
        parts = [(above_west, high, west), (above_east, high, east), (below_west, low, west), (below_east, low, east)]
    else:
        parts = [(above, high, inside), (below, low, inside)]
    half = len(parts) // 2
    source = block if second else fields
    moves = [(ref, ext.at[:, rows, cols]) for ref, rows, cols in parts[:half]]
    moves += [(source.at[:, i], ext.at[:, 2 + i, inside]) for i in range(ROWS)]
    moves += [(ref, ext.at[:, rows, cols]) for ref, rows, cols in parts[half:]]
    if second:
        moves += [(fields.at[:, i], base.at[:, i]) for i in range(ROWS)]
    copies = [pltpu.make_async_copy(ref, into, sems.at[n]) for n, (ref, into) in enumerate(moves)]
    for copy in copies:
        copy.start()
    needed = [copies[: half + 3], [copies[half + 3]], copies[half + 4 : 2 * half + 4], []]
    if second:
        needed = [list(some) + [copies[2 * half + 4 + i]] for i, some in enumerate(needed)]
    send[...] = jnp.zeros_like(send)
    west_edge, east_edge = edge[2] > 0, edge[3] > 0
    for f in range(FIELDS):
        for i in range(ROWS):
            pair = slice(2 * i, 2 * i + 2)
            ext[f, 2 + i, PAD - 2 : PAD, :] = jnp.where(west_edge, 0.0, before[f, pair, :])
            ext[f, 2 + i, PAD + COLS : PAD + COLS + 2, :] = jnp.where(east_edge, 0.0, after[f, pair, :])

    def finish(n):
        start, fix = ((0, fix_above), (6, fix_below))[n] if second else (6 * n, None)
        if second:
            for f in range(FIELDS):
                for i in range(HALF):
                    ext[f, start + i, PAD : PAD + 2, :] = fix[f, 4 * i : 4 * i + 2, :]
                    ext[f, start + i, PAD + COLS - 2 : PAD + COLS, :] = fix[f, 4 * i + 2 : 4 * i + 4, :]

        @pl.when(edge[n] > 0)
        def _():
            ext[:, start : start + HALF] = jnp.zeros((FIELDS, HALF, EXT, SHELLS), jnp.float32)

    lane = lax.broadcasted_iota(jnp.int32, (8, SHELLS), 1)
    first, second_lane = lane < 1, lane < 2
    last, before_last = lane > SHELLS - 2, lane > SHELLS - 3
    inv_r = inv_r_ref[...]
    k_r = 1.0 / (12.0 * RADIAL_STEP)
    g_t = inv_r * (1.0 / (12.0 * THETA_STEP))

    def d_r(x):
        near_low = jnp.where(first, x, pltpu.roll(x, 1, 1))
        far_low = jnp.where(second_lane, near_low, pltpu.roll(x, 2, 1))
        near_high = jnp.where(last, x, pltpu.roll(x, SHELLS - 1, 1))
        far_high = jnp.where(before_last, near_high, pltpu.roll(x, SHELLS - 2, 1))
        return diff(far_low, near_low, near_high, far_high) * k_r

    for i in range(ROWS):
        for copy in needed[i]:
            copy.wait()
        if i in (0, 2):
            finish(i // 2)
        sine, cosine, cot, inv_sine = [row_const[i, k] for k in range(4)]
        omega_y, omega_z = row_const[i, 4], row_const[i, 5]
        g_p = inv_r * (inv_sine * (1.0 / (12.0 * PHI_STEP)))
        cot_r = inv_r * cot

        def tile(j, carry):
            start = pl.multiple_of(j * 8, 8)
            rows = pl.ds(start, 8)
            padded = pl.ds(pl.multiple_of(start + PAD, 8), 8)
            q, ur, ut, up, h, br, bt, bp = [ext[f, 2 + i, padded, :] for f in range(FIELDS)]
            near = [[ext[f, 2 + i + d, padded, :] for f in range(FIELDS)] for d in (-2, -1, 1, 2)]
            tq, tur, tut, tup, th, tbr, _, tbp = [
                diff(*[n[f] for n in near]) * g_t if f != 6 else None for f in range(FIELDS)
            ]
            t_er = diff(*[n[2] * n[7] - n[3] * n[6] for n in near]) * g_t
            t_ep = diff(*[n[1] * n[6] - n[2] * n[5] for n in near]) * g_t
            near = [[ext[f, 2 + i, pl.ds(start + (PAD + d), 8), :] for f in range(FIELDS)] for d in (-2, -1, 1, 2)]
            pq, pur, put, pup, ph, pbr, pbt, _ = [
                diff(*[n[f] for n in near]) * g_p if f != 7 else None for f in range(FIELDS)
            ]
            p_er = diff(*[n[2] * n[7] - n[3] * n[6] for n in near]) * g_p
            p_et = diff(*[n[3] * n[5] - n[1] * n[7] for n in near]) * g_p
            er = ut * bp - up * bt
            et = up * br - ur * bp
            ep = ur * bt - ut * br
            rq, rur, rut, rup, rh, rbt, rbp, r_et, r_ep = [d_r(x) for x in (q, ur, ut, up, h, bt, bp, et, ep)]

            div = rur + 2.0 * ur * inv_r + tut + cot_r * ut + pup
            cur_r = tbp + cot_r * bp - pbt
            cur_t = pbr - rbp - bp * inv_r
            cur_p = rbt + bt * inv_r - tbr
            sin_phi = phi_const[0, rows, :]
            cos_phi = phi_const[1, rows, :]
            w_r = (omega_y * sine) * sin_phi + omega_z * cosine
            w_t = (omega_y * cosine) * sin_phi - omega_z * sine
            w_p = omega_y * cos_phi
            inv_rho = jnp.exp(-q)
            temper = jnp.exp(h - q)

            def adv(gr, gt, gp):
                return ur * gr + ut * gt + up * gp

            rates = [
                -adv(rq, tq, pq) - div,
                -adv(rur, tur, pur)
                + (ut * ut + up * up) * inv_r
                - temper * rh
                + inv_rho * (cur_t * bp - cur_p * bt)
                - 2.0 * (w_t * up - w_p * ut)
                - gravity * inv_r * inv_r,
                -adv(rut, tut, put)
                - (ur * ut * inv_r - cot_r * (up * up))
                - temper * th
                + inv_rho * (cur_p * br - cur_r * bp)
                - 2.0 * (w_p * ur - w_r * up),
                -adv(rup, tup, pup)
                - (ur * up * inv_r + cot_r * (ut * up))
                - temper * ph
                + inv_rho * (cur_r * bt - cur_t * br)
                - 2.0 * (w_r * ut - w_t * ur),
                -adv(rh, th, ph) - gamma_ratio * div,
                t_ep + cot_r * ep - p_et,
                p_er - r_ep - ep * inv_r,
                r_et + et * inv_r - t_er,
            ]
            centre = [q, ur, ut, up, h, br, bt, bp]
            for f in range(FIELDS):
                if second:
                    value = 0.5 * (base[f, i, rows, :] + centre[f] + time_step * rates[f])
                else:
                    value = centre[f] + time_step * rates[f]
                new[f, i, rows, :] = value
            return carry

        lax.fori_loop(0, COLS // 8, tile, 0, unroll=4)

    leaving = []
    if not second:
        for n, piece in enumerate(pieces):
            cols = (pl.ds(0, EARLY), pl.ds(EARLY, COLS - EARLY))[n % 2]
            part = new.at[:, pl.ds(HALF * (n // 2), HALF), cols]
            leaving.append(pltpu.make_async_copy(part, piece, sems.at[12 + n]))
            leaving[-1].start()

    values = []
    for f in range(0, FIELDS, 2):
        pair = jnp.concatenate([new[f + n].reshape(CELLS, SHELLS) for n in range(2)], axis=1)
        both = jnp.dot(
            corner[...], pair, precision=lax.Precision.HIGHEST, preferred_element_type=jnp.float32
        )
        values += [both[:, :SHELLS], both[:, SHELLS:]]
    c, s = angle[0], angle[1]
    for t, p in ((2, 3), (6, 7)):
        values[t], values[p] = c * values[t] - s * values[p], s * values[t] + c * values[p]
    donor[...] = jnp.swapaxes(jnp.stack(values), 0, 1)

    for m in range(0, SLOTS, 16):
        spots = [place[m + k] for k in range(16)]
        columns = [donor[m + k] for k in range(16)]
        for spot, column in zip(spots, columns):
            send[spot] = column
    near_send[...] = send[:PARCEL]
    far_send[...] = send[PARCEL:]
    for copy in leaving:
        copy.wait()


def run_step(second, args):
    pieces = () if second else tuple(struct(FIELDS, HALF, n, SHELLS) for n in (EARLY, COLS - EARLY)) * 2
    return pl.pallas_call(
        lambda *refs: step_kernel(second, *refs),
        out_shape=(struct(*BLOCK), *pieces) + (struct(PARCEL, FIELDS, SHELLS),) * 2,
        in_specs=([VMEM] * 2 + [ANY] * 5 if second else [ANY] * 2)
        + [ANY]
        + [VMEM] * 2
        + [SMEM] * 2
        + [VMEM] * 4
        + [SMEM],
        out_specs=(VMEM,) + (ANY,) * len(pieces) + (VMEM,) * 2,
        scratch_shapes=[
            pltpu.VMEM((FIELDS, ROWS + 4, EXT, SHELLS), jnp.float32),
            pltpu.VMEM((SLOTS, FIELDS, SHELLS), jnp.float32),
            pltpu.VMEM((2 * PARCEL, FIELDS, SHELLS), jnp.float32),
            pltpu.VMEM((FIELDS, ROWS if second else 1, COLS, SHELLS), jnp.float32),
            pltpu.SemaphoreType.DMA((16,)),
        ],
        compiler_params=params(20),
    )(*args)


def sort_kernel(near, far, mate_near, mate_far, core, chunks):
    for n, ref in enumerate((near, far, mate_near, mate_far)):
        for k in range(2):
            own = 2 * core[0] + k
            chunks[0, 2 * n + k] = ref[own]
            chunks[N_THETA - 1, 2 * n + k] = ref[PARCEL - 4 + own]
            for row in range(1, N_THETA - 1):
                chunks[row, 2 * n + k] = ref[2 + 2 * row + k]


def run_sort(*args):
    return pl.pallas_call(
        sort_kernel,
        out_shape=struct(N_THETA, CHUNK, FIELDS, SHELLS),
        in_specs=[VMEM] * 4 + [SMEM],
        out_specs=VMEM,
        compiler_params=params(8),
    )(*args)


def merge_kernel(last, block, moved, pick, mean, merged, *refs):
    kept, gathered, sems = refs[-3:]
    copy = pltpu.make_async_copy(block, kept, sems.at[0])
    leaving = []
    copy.start()
    columns = jnp.swapaxes(moved[...], 0, 1)
    for f in range(FIELDS):
        gathered[f // 2, :, f % 2 * SHELLS : (f % 2 + 1) * SHELLS] = columns[f]
    copy.wait()
    weight = mean[...]
    for pair in range(FIELDS // 2):
        parts = thirds(gathered[pair])
        total = sum(jnp.dot(pick[...], x, preferred_element_type=jnp.float32) for x in parts)
        for n in range(2):
            f = 2 * pair + n
            average = total[:, n * SHELLS : (n + 1) * SHELLS] * weight
            result = jnp.where(weight > 0.0, average, kept[f].reshape(CELLS, SHELLS))
            if last:
                kept[f] = result.reshape(ROWS, COLS, SHELLS)
            else:
                merged[f] = result.reshape(ROWS, COLS, SHELLS)
        if last:
            fields = pl.ds(2 * pair, 2)
            leaving.append(pltpu.make_async_copy(kept.at[fields], merged.at[fields], sems.at[1 + pair]))
            leaving[-1].start()
    for copy in leaving:
        copy.wait()
    if not last:
        west, east, head, foot = refs[:4]
        store_rims(merged, west, east, COLS)
        for f in range(FIELDS):
            for i in range(HALF):
                for row, fix in ((i, head), (HALF + i, foot)):
                    fix[f, 4 * i : 4 * i + 2, :] = merged[f, row, :2, :]
                    fix[f, 4 * i + 2 : 4 * i + 4, :] = merged[f, row, COLS - 2 :, :]


def run_merge(last, *args):
    shapes = (struct(*BLOCK),) + (() if last else (struct(*RIM),) * 4)
    return pl.pallas_call(
        lambda *refs: merge_kernel(last, *refs),
        out_shape=shapes,
        in_specs=[ANY] + [VMEM] * 3,
        out_specs=(ANY if last else VMEM,) + (VMEM,) * (len(shapes) - 1),
        scratch_shapes=[
            pltpu.VMEM(BLOCK, jnp.float32),
            pltpu.VMEM((FIELDS // 2, N_THETA * CHUNK, 2 * SHELLS), jnp.float32),
            pltpu.SemaphoreType.DMA((5,)),
        ],
        compiler_params=params(16),
    )(*args)


def shift(x, axis, size, by):
    return lax.ppermute(x, axis, [(i, (i + by) % size) for i in range(size)])


def local(fields, donor_base, weights, frame_angle, destination, target_cell):
    own = fields[0]
    patch, ti, pi = [lax.axis_index(axis) for axis in EVERYONE]

    top, bottom, west, east = run_split(own)
    above, below = shift(bottom, "theta", N_THETA, 1), shift(top, "theta", N_THETA, -1)
    before, after = shift(east, "phi", N_PHI, 1), shift(west, "phi", N_PHI, -1)
    edge = jnp.stack([ti == 0, ti == N_THETA - 1, pi == 0, pi == N_PHI - 1]).astype(jnp.int32)

    row_index = ti * ROWS + jnp.arange(ROWS, dtype=jnp.int32)
    theta = 0.25 * math.pi - margin + (row_index.astype(jnp.float32) + 0.5) * THETA_STEP
    col_index = pi * COLS + jnp.arange(COLS, dtype=jnp.int32)
    phi = -0.75 * math.pi - margin + (col_index.astype(jnp.float32) + 0.5) * PHI_STEP
    flag = patch.astype(jnp.float32)
    sine, cosine = jnp.sin(theta), jnp.cos(theta)
    ones = jnp.ones_like(sine)
    row_const = jnp.stack(
        [sine, cosine, cosine / sine, 1.0 / sine, ones * (rotation * flag), ones * (rotation * (1.0 - flag))], axis=1
    )
    phi_const = jnp.broadcast_to(jnp.stack([jnp.sin(phi), jnp.cos(phi)])[:, :, None], (2, COLS, SHELLS))
    radius = inner_radius + RADIAL_STEP * (jnp.arange(SHELLS, dtype=jnp.int32).astype(jnp.float32) + 0.5)
    inv_r = jnp.broadcast_to((1.0 / radius)[None, :], (8, SHELLS))

    base = donor_base[0, 0, 0]
    first = base // (COLS - 1) * COLS + base % (COLS - 1)
    w = weights[0, 0, 0]
    cells = jnp.arange(CELLS, dtype=jnp.int32)[None, :]
    corner = sum(
        jnp.where(cells == (first + offset)[:, None], w[k][:, None], 0.0)
        for k, offset in enumerate((0, 1, COLS, COLS + 1))
    )
    angle = frame_angle[0, 0, 0]
    angle = jnp.broadcast_to(jnp.stack([jnp.cos(angle), jnp.sin(angle)])[:, :, None], (2, SLOTS, SHELLS))

    receiver = destination[0, 0, 0]
    slot = jnp.arange(SLOTS, dtype=jnp.int32)
    rank = jnp.sum(
        ((receiver[:, None] == receiver[None, :]) & (slot[None, :] < slot[:, None])).astype(jnp.int32), axis=1
    )
    to_row, to_col = receiver // N_PHI, receiver % N_PHI
    end_spot = 2 * (to_col % 2) + rank
    spot = jnp.where(
        to_row == 0, end_spot, jnp.where(to_row == N_THETA - 1, PARCEL - 4 + end_spot, 2 + 2 * to_row + rank)
    )
    place = jnp.where(to_col // 2 == pi // 2, spot, PARCEL + spot)
    core = (pi % 2).astype(jnp.int32).reshape(1)

    def across(x, by):
        pairs = [(a * N_PHI + p, (1 - a) * N_PHI + (p + by) % N_PHI) for a in range(2) for p in range(N_PHI)]
        return lax.ppermute(x, ("patch", "phi"), pairs)

    def gather_pair(near, far):
        near, far = across(near, 0), across(far, 2)
        swap = [(0, 1), (1, 0), (2, 3), (3, 2)]
        return near, far, lax.ppermute(near, "phi", swap), lax.ppermute(far, "phi", swap)

    def exchange(near, far, *first):
        chunks = run_sort(*gather_pair(near, far), core)
        chunks, first = lax.optimization_barrier((chunks, first))
        chunks = chunks.reshape(N_THETA, CHUNK * FIELDS, SHELLS)
        moved = lax.all_to_all(chunks, "theta", 0, 0, tiled=True)
        return moved.reshape(N_THETA * CHUNK, FIELDS, SHELLS), *first

    def exchange_ids(sent):
        lanes = [jnp.pad(sent[n * PARCEL : (n + 1) * PARCEL], (0, SHELLS - PARCEL))[None] for n in range(2)]
        parts = jnp.concatenate(gather_pair(*lanes))
        inside = parts[:, 4 : PARCEL - 4].reshape(4, N_THETA - 2, 2)
        first = lax.dynamic_slice_in_dim(parts, 2 * core[0], 2, 1)[:, None]
        final = lax.dynamic_slice_in_dim(parts, PARCEL - 4 + 2 * core[0], 2, 1)[:, None]
        chunks = jnp.concatenate([first, inside, final], axis=1).swapaxes(0, 1).reshape(N_THETA, 1, CHUNK)
        chunks = jnp.pad(chunks, ((0, 0), (0, 0), (0, SHELLS - CHUNK)))
        moved = lax.all_to_all(chunks, "theta", 0, 0, tiled=True)
        return moved[:, 0, :CHUNK].reshape(N_THETA * CHUNK)

    position = jnp.arange(2 * PARCEL, dtype=jnp.int32)
    target = target_cell[0, 0, 0]
    sent = jnp.sum(jnp.where(position[:, None] == place[None, :], target[None, :] + 1, 0), axis=1) - 1
    sent, _ = lax.optimization_barrier((sent, (before, after)))
    ids = jnp.where(jnp.sum(edge) > 0, exchange_ids(sent), -1)
    picked = ids[None, :] == jnp.arange(CELLS, dtype=jnp.int32)[:, None]
    pick = picked.astype(jnp.bfloat16)
    count = jnp.sum(picked.astype(jnp.float32), axis=1)
    mean = jnp.where(count > 0.0, 1.0 / jnp.maximum(count, 1.0), 0.0)
    mean = jnp.broadcast_to(mean[:, None], (CELLS, SHELLS))

    edge, pick = lax.optimization_barrier((edge, pick))
    tail = (edge, row_const, phi_const, inv_r, corner, angle, place)
    block, *pieces, near, far = run_step(False, (above, below, own, before, after, *tail))
    above_west, above_east = [shift(x, "theta", N_THETA, 1) for x in pieces[2:]]
    below_west, below_east = [shift(x, "theta", N_THETA, -1) for x in pieces[:2]]
    moved, above_west, below_west = exchange(near, far, above_west, below_west)
    block, west, east, head, foot = run_merge(False, block, moved, pick, mean)
    fixes = shift(foot, "theta", N_THETA, 1), shift(head, "theta", N_THETA, -1)
    before, after = shift(east, "phi", N_PHI, 1), shift(west, "phi", N_PHI, -1)
    halo = (above_west, above_east, below_west, below_east)
    block, near, far = run_step(True, (*fixes, block, *halo, own, before, after, *tail))
    (result,) = run_merge(True, block, *exchange(near, far), pick, mean)
    return result[None]


def solution(mesh):
    placed = (
        P("patch", None, "theta", "phi", None),
        P("patch", "theta", "phi", None),
        P("patch", "theta", "phi", None, None),
        P("patch", "theta", "phi", None),
        P("patch", "theta", "phi", None),
        P("patch", "theta", "phi", None),
    )
    return jax.shard_map(
        local,
        mesh=mesh,
        in_specs=placed,
        out_specs=P("patch", None, "theta", "phi", None),
        check_vma=False,
    )
```

```python
import math

import jax
import jax.numpy as jnp
from jax import lax
from jax.experimental import pallas as pl
from jax.experimental.pallas import tpu as pltpu
from jax.sharding import PartitionSpec as P

margin = 0.03
inner_radius = 0.35
outer_radius = 1.0
gamma_ratio = 5.0 / 3.0
gravity = 1.0
rotation = 2.0
time_step = 0.002

ROWS, COLS, SHELLS, FIELDS, SLOTS = 4, 128, 128, 8, 96
HALF = ROWS // 2
CELLS = ROWS * COLS
N_THETA, N_PHI = 32, 4
DEVS = N_THETA * N_PHI
PAD = 8
EXT = COLS + 2 * PAD
THETA_STEP = (0.5 * math.pi + 2.0 * margin) / (ROWS * N_THETA)
PHI_STEP = (1.5 * math.pi + 2.0 * margin) / (COLS * N_PHI)
RADIAL_STEP = (outer_radius - inner_radius) / SHELLS
VMEM = pl.BlockSpec(memory_space=pltpu.VMEM)
SMEM = pl.BlockSpec(memory_space=pltpu.SMEM)
ANY = pl.BlockSpec(memory_space=pl.ANY)
EVERYONE = ("patch", "theta", "phi")


def struct(*shape):
    return jax.ShapeDtypeStruct(shape, jnp.float32)


BLOCK = (FIELDS, ROWS, COLS, SHELLS)
HALF_BLOCK = (FIELDS, HALF, COLS, SHELLS)
EARLY = 48
RIM = (FIELDS, 8, SHELLS)
PARCEL = 2 * N_THETA + 4
CHUNK = 8


def params(mib):
    return pltpu.CompilerParams(vmem_limit_bytes=mib * 1024 * 1024)


def store_rims(block, west, east, width):
    for f in range(FIELDS):
        for i in range(ROWS):
            west[f, 2 * i : 2 * i + 2, :] = block[f, i, :2, :]
            east[f, 2 * i : 2 * i + 2, :] = block[f, i, width - 2 : width, :]


def split_kernel(fields, top, bottom, west, east, rims, sems):
    copies = [
        pltpu.make_async_copy(fields.at[:, :, :8], rims.at[:, :, :8], sems.at[0]),
        pltpu.make_async_copy(fields.at[:, :, COLS - 8 :], rims.at[:, :, 8:], sems.at[1]),
        pltpu.make_async_copy(fields.at[:, :HALF], top, sems.at[2]),
        pltpu.make_async_copy(fields.at[:, HALF:], bottom, sems.at[3]),
    ]
    for copy in copies:
        copy.start()
    for copy in copies[:2]:
        copy.wait()
    store_rims(rims, west, east, 16)
    for copy in copies[2:]:
        copy.wait()


def run_split(fields):
    return pl.pallas_call(
        split_kernel,
        out_shape=(struct(*HALF_BLOCK), struct(*HALF_BLOCK), struct(*RIM), struct(*RIM)),
        in_specs=[ANY],
        out_specs=(ANY, ANY, VMEM, VMEM),
        scratch_shapes=[pltpu.VMEM((FIELDS, ROWS, 16, SHELLS), jnp.float32), pltpu.SemaphoreType.DMA((4,))],
        compiler_params=params(8),
    )(fields)


def thirds(x):
    high = x.astype(jnp.bfloat16)
    rest = x - high.astype(jnp.float32)
    middle = rest.astype(jnp.bfloat16)
    return (rest - middle.astype(jnp.float32)).astype(jnp.bfloat16), middle, high


def diff(far_low, near_low, near_high, far_high):
    return (far_low - far_high) + 8.0 * (near_high - near_low)


def step_kernel(second, *refs):
    if second:
        fix_above, fix_below, block, above_west, above_east, below_west, below_east, *refs = refs
    else:
        above, below, *refs = refs
    fields, before, after, edge, row_const, phi_const, inv_r_ref, corner, angle, place, new, *refs = refs
    if not second:
        pieces, refs = refs[:4], refs[4:]
    near_send, far_send, ext, donor, send, base, sems = refs
    west, east, inside = pl.ds(PAD, EARLY), pl.ds(PAD + EARLY, COLS - EARLY), pl.ds(PAD, COLS)
    high, low = slice(0, HALF), slice(ROWS + 2, ROWS + 2 + HALF)
    if second:
        parts = [(above_west, high, west), (above_east, high, east), (below_west, low, west), (below_east, low, east)]
    else:
        parts = [(above, high, inside), (below, low, inside)]
    half = len(parts) // 2
    source = block if second else fields
    moves = [(ref, ext.at[:, rows, cols]) for ref, rows, cols in parts[:half]]
    moves += [(source.at[:, i], ext.at[:, 2 + i, inside]) for i in range(ROWS)]
    moves += [(ref, ext.at[:, rows, cols]) for ref, rows, cols in parts[half:]]
    if second:
        moves += [(fields.at[:, i], base.at[:, i]) for i in range(ROWS)]
    copies = [pltpu.make_async_copy(ref, into, sems.at[n]) for n, (ref, into) in enumerate(moves)]
    for copy in copies:
        copy.start()
    needed = [copies[: half + 3], [copies[half + 3]], copies[half + 4 : 2 * half + 4], []]
    if second:
        needed = [list(some) + [copies[2 * half + 4 + i]] for i, some in enumerate(needed)]
    send[...] = jnp.zeros_like(send)
    west_edge, east_edge = edge[2] > 0, edge[3] > 0
    for f in range(FIELDS):
        for i in range(ROWS):
            pair = slice(2 * i, 2 * i + 2)
            ext[f, 2 + i, PAD - 2 : PAD, :] = jnp.where(west_edge, 0.0, before[f, pair, :])
            ext[f, 2 + i, PAD + COLS : PAD + COLS + 2, :] = jnp.where(east_edge, 0.0, after[f, pair, :])

    def finish(n):
        start, fix = ((0, fix_above), (6, fix_below))[n] if second else (6 * n, None)
        if second:
            for f in range(FIELDS):
                for i in range(HALF):
                    ext[f, start + i, PAD : PAD + 2, :] = fix[f, 4 * i : 4 * i + 2, :]
                    ext[f, start + i, PAD + COLS - 2 : PAD + COLS, :] = fix[f, 4 * i + 2 : 4 * i + 4, :]

        @pl.when(edge[n] > 0)
        def _():
            ext[:, start : start + HALF] = jnp.zeros((FIELDS, HALF, EXT, SHELLS), jnp.float32)

    lane = lax.broadcasted_iota(jnp.int32, (8, SHELLS), 1)
    first, second_lane = lane < 1, lane < 2
    last, before_last = lane > SHELLS - 2, lane > SHELLS - 3
    inv_r = inv_r_ref[...]
    k_r = 1.0 / (12.0 * RADIAL_STEP)
    g_t = inv_r * (1.0 / (12.0 * THETA_STEP))

    def d_r(x):
        near_low = jnp.where(first, x, pltpu.roll(x, 1, 1))
        far_low = jnp.where(second_lane, near_low, pltpu.roll(x, 2, 1))
        near_high = jnp.where(last, x, pltpu.roll(x, SHELLS - 1, 1))
        far_high = jnp.where(before_last, near_high, pltpu.roll(x, SHELLS - 2, 1))
        return diff(far_low, near_low, near_high, far_high) * k_r

    for i in range(ROWS):
        for copy in needed[i]:
            copy.wait()
        if i in (0, 2):
            finish(i // 2)
        sine, cosine, cot, inv_sine = [row_const[i, k] for k in range(4)]
        omega_y, omega_z = row_const[i, 4], row_const[i, 5]
        g_p = inv_r * (inv_sine * (1.0 / (12.0 * PHI_STEP)))
        cot_r = inv_r * cot

        def tile(j, carry):
            start = pl.multiple_of(j * 8, 8)
            rows = pl.ds(start, 8)
            padded = pl.ds(pl.multiple_of(start + PAD, 8), 8)
            q, ur, ut, up, h, br, bt, bp = [ext[f, 2 + i, padded, :] for f in range(FIELDS)]
            near = [[ext[f, 2 + i + d, padded, :] for f in range(FIELDS)] for d in (-2, -1, 1, 2)]
            tq, tur, tut, tup, th, tbr, _, tbp = [
                diff(*[n[f] for n in near]) * g_t if f != 6 else None for f in range(FIELDS)
            ]
            t_er = diff(*[n[2] * n[7] - n[3] * n[6] for n in near]) * g_t
            t_ep = diff(*[n[1] * n[6] - n[2] * n[5] for n in near]) * g_t
            near = [[ext[f, 2 + i, pl.ds(start + (PAD + d), 8), :] for f in range(FIELDS)] for d in (-2, -1, 1, 2)]
            pq, pur, put, pup, ph, pbr, pbt, _ = [
                diff(*[n[f] for n in near]) * g_p if f != 7 else None for f in range(FIELDS)
            ]
            p_er = diff(*[n[2] * n[7] - n[3] * n[6] for n in near]) * g_p
            p_et = diff(*[n[3] * n[5] - n[1] * n[7] for n in near]) * g_p
            er = ut * bp - up * bt
            et = up * br - ur * bp
            ep = ur * bt - ut * br
            rq, rur, rut, rup, rh, rbt, rbp, r_et, r_ep = [d_r(x) for x in (q, ur, ut, up, h, bt, bp, et, ep)]

            div = rur + 2.0 * ur * inv_r + tut + cot_r * ut + pup
            cur_r = tbp + cot_r * bp - pbt
            cur_t = pbr - rbp - bp * inv_r
            cur_p = rbt + bt * inv_r - tbr
            sin_phi = phi_const[0, rows, :]
            cos_phi = phi_const[1, rows, :]
            w_r = (omega_y * sine) * sin_phi + omega_z * cosine
            w_t = (omega_y * cosine) * sin_phi - omega_z * sine
            w_p = omega_y * cos_phi
            inv_rho = jnp.exp(-q)
            temper = jnp.exp(h - q)

            def adv(gr, gt, gp):
                return ur * gr + ut * gt + up * gp

            rates = [
                -adv(rq, tq, pq) - div,
                -adv(rur, tur, pur)
                + (ut * ut + up * up) * inv_r
                - temper * rh
                + inv_rho * (cur_t * bp - cur_p * bt)
                - 2.0 * (w_t * up - w_p * ut)
                - gravity * inv_r * inv_r,
                -adv(rut, tut, put)
                - (ur * ut * inv_r - cot_r * (up * up))
                - temper * th
                + inv_rho * (cur_p * br - cur_r * bp)
                - 2.0 * (w_p * ur - w_r * up),
                -adv(rup, tup, pup)
                - (ur * up * inv_r + cot_r * (ut * up))
                - temper * ph
                + inv_rho * (cur_r * bt - cur_t * br)
                - 2.0 * (w_r * ut - w_t * ur),
                -adv(rh, th, ph) - gamma_ratio * div,
                t_ep + cot_r * ep - p_et,
                p_er - r_ep - ep * inv_r,
                r_et + et * inv_r - t_er,
            ]
            centre = [q, ur, ut, up, h, br, bt, bp]
            for f in range(FIELDS):
                if second:
                    value = 0.5 * (base[f, i, rows, :] + centre[f] + time_step * rates[f])
                else:
                    value = centre[f] + time_step * rates[f]
                new[f, i, rows, :] = value
            return carry

        lax.fori_loop(0, COLS // 8, tile, 0, unroll=8)

    leaving = []
    if not second:
        for n, piece in enumerate(pieces):
            cols = (pl.ds(0, EARLY), pl.ds(EARLY, COLS - EARLY))[n % 2]
            part = new.at[:, pl.ds(HALF * (n // 2), HALF), cols]
            leaving.append(pltpu.make_async_copy(part, piece, sems.at[12 + n]))
            leaving[-1].start()

    values = []
    for f in range(0, FIELDS, 2):
        pair = jnp.concatenate([new[f + n].reshape(CELLS, SHELLS) for n in range(2)], axis=1)
        both = jnp.dot(
            corner[...], pair, precision=lax.Precision.HIGHEST, preferred_element_type=jnp.float32
        )
        values += [both[:, :SHELLS], both[:, SHELLS:]]
    c, s = angle[0], angle[1]
    for t, p in ((2, 3), (6, 7)):
        values[t], values[p] = c * values[t] - s * values[p], s * values[t] + c * values[p]
    donor[...] = jnp.swapaxes(jnp.stack(values), 0, 1)

    for m in range(0, SLOTS, 16):
        spots = [place[m + k] for k in range(16)]
        columns = [donor[m + k] for k in range(16)]
        for spot, column in zip(spots, columns):
            send[spot] = column
    near_send[...] = send[:PARCEL]
    far_send[...] = send[PARCEL:]
    for copy in leaving:
        copy.wait()


def run_step(second, args):
    pieces = () if second else tuple(struct(FIELDS, HALF, n, SHELLS) for n in (EARLY, COLS - EARLY)) * 2
    return pl.pallas_call(
        lambda *refs: step_kernel(second, *refs),
        out_shape=(struct(*BLOCK), *pieces) + (struct(PARCEL, FIELDS, SHELLS),) * 2,
        in_specs=([VMEM] * 2 + [ANY] * 5 if second else [ANY] * 2)
        + [ANY]
        + [VMEM] * 2
        + [SMEM] * 2
        + [VMEM] * 4
        + [SMEM],
        out_specs=(VMEM,) + (ANY,) * len(pieces) + (VMEM,) * 2,
        scratch_shapes=[
            pltpu.VMEM((FIELDS, ROWS + 4, EXT, SHELLS), jnp.float32),
            pltpu.VMEM((SLOTS, FIELDS, SHELLS), jnp.float32),
            pltpu.VMEM((2 * PARCEL, FIELDS, SHELLS), jnp.float32),
            pltpu.VMEM((FIELDS, ROWS if second else 1, COLS, SHELLS), jnp.float32),
            pltpu.SemaphoreType.DMA((16,)),
        ],
        compiler_params=params(20),
    )(*args)


def sort_kernel(near, far, mate_near, mate_far, core, chunks):
    for n, ref in enumerate((near, far, mate_near, mate_far)):
        for k in range(2):
            own = 2 * core[0] + k
            chunks[0, 2 * n + k] = ref[own]
            chunks[N_THETA - 1, 2 * n + k] = ref[PARCEL - 4 + own]
            for row in range(1, N_THETA - 1):
                chunks[row, 2 * n + k] = ref[2 + 2 * row + k]


def run_sort(*args):
    return pl.pallas_call(
        sort_kernel,
        out_shape=struct(N_THETA, CHUNK, FIELDS, SHELLS),
        in_specs=[VMEM] * 4 + [SMEM],
        out_specs=VMEM,
        compiler_params=params(8),
    )(*args)


def merge_kernel(last, block, moved, pick, mean, merged, *refs):
    kept, gathered, sems = refs[-3:]
    copy = pltpu.make_async_copy(block, kept, sems.at[0])
    leaving = []
    copy.start()
    columns = jnp.swapaxes(moved[...], 0, 1)
    for f in range(FIELDS):
        gathered[f // 2, :, f % 2 * SHELLS : (f % 2 + 1) * SHELLS] = columns[f]
    copy.wait()
    weight = mean[...]
    for pair in range(FIELDS // 2):
        parts = thirds(gathered[pair])
        total = sum(jnp.dot(pick[...], x, preferred_element_type=jnp.float32) for x in parts)
        for n in range(2):
            f = 2 * pair + n
            average = total[:, n * SHELLS : (n + 1) * SHELLS] * weight
            result = jnp.where(weight > 0.0, average, kept[f].reshape(CELLS, SHELLS))
            if last:
                kept[f] = result.reshape(ROWS, COLS, SHELLS)
            else:
                merged[f] = result.reshape(ROWS, COLS, SHELLS)
        if last:
            fields = pl.ds(2 * pair, 2)
            leaving.append(pltpu.make_async_copy(kept.at[fields], merged.at[fields], sems.at[1 + pair]))
            leaving[-1].start()
    for copy in leaving:
        copy.wait()
    if not last:
        west, east, head, foot = refs[:4]
        store_rims(merged, west, east, COLS)
        for f in range(FIELDS):
            for i in range(HALF):
                for row, fix in ((i, head), (HALF + i, foot)):
                    fix[f, 4 * i : 4 * i + 2, :] = merged[f, row, :2, :]
                    fix[f, 4 * i + 2 : 4 * i + 4, :] = merged[f, row, COLS - 2 :, :]


def run_merge(last, *args):
    shapes = (struct(*BLOCK),) + (() if last else (struct(*RIM),) * 4)
    return pl.pallas_call(
        lambda *refs: merge_kernel(last, *refs),
        out_shape=shapes,
        in_specs=[ANY] + [VMEM] * 3,
        out_specs=(ANY if last else VMEM,) + (VMEM,) * (len(shapes) - 1),
        scratch_shapes=[
            pltpu.VMEM(BLOCK, jnp.float32),
            pltpu.VMEM((FIELDS // 2, N_THETA * CHUNK, 2 * SHELLS), jnp.float32),
            pltpu.SemaphoreType.DMA((5,)),
        ],
        compiler_params=params(16),
    )(*args)


def shift(x, axis, size, by):
    return lax.ppermute(x, axis, [(i, (i + by) % size) for i in range(size)])


def local(fields, donor_base, weights, frame_angle, destination, target_cell):
    own = fields[0]
    patch, ti, pi = [lax.axis_index(axis) for axis in EVERYONE]

    top, bottom, west, east = run_split(own)
    above, below = shift(bottom, "theta", N_THETA, 1), shift(top, "theta", N_THETA, -1)
    before, after = shift(east, "phi", N_PHI, 1), shift(west, "phi", N_PHI, -1)
    edge = jnp.stack([ti == 0, ti == N_THETA - 1, pi == 0, pi == N_PHI - 1]).astype(jnp.int32)

    row_index = ti * ROWS + jnp.arange(ROWS, dtype=jnp.int32)
    theta = 0.25 * math.pi - margin + (row_index.astype(jnp.float32) + 0.5) * THETA_STEP
    col_index = pi * COLS + jnp.arange(COLS, dtype=jnp.int32)
    phi = -0.75 * math.pi - margin + (col_index.astype(jnp.float32) + 0.5) * PHI_STEP
    flag = patch.astype(jnp.float32)
    sine, cosine = jnp.sin(theta), jnp.cos(theta)
    ones = jnp.ones_like(sine)
    row_const = jnp.stack(
        [sine, cosine, cosine / sine, 1.0 / sine, ones * (rotation * flag), ones * (rotation * (1.0 - flag))], axis=1
    )
    phi_const = jnp.broadcast_to(jnp.stack([jnp.sin(phi), jnp.cos(phi)])[:, :, None], (2, COLS, SHELLS))
    radius = inner_radius + RADIAL_STEP * (jnp.arange(SHELLS, dtype=jnp.int32).astype(jnp.float32) + 0.5)
    inv_r = jnp.broadcast_to((1.0 / radius)[None, :], (8, SHELLS))

    base = donor_base[0, 0, 0]
    first = base // (COLS - 1) * COLS + base % (COLS - 1)
    w = weights[0, 0, 0]
    cells = jnp.arange(CELLS, dtype=jnp.int32)[None, :]
    corner = sum(
        jnp.where(cells == (first + offset)[:, None], w[k][:, None], 0.0)
        for k, offset in enumerate((0, 1, COLS, COLS + 1))
    )
    angle = frame_angle[0, 0, 0]
    angle = jnp.broadcast_to(jnp.stack([jnp.cos(angle), jnp.sin(angle)])[:, :, None], (2, SLOTS, SHELLS))

    receiver = destination[0, 0, 0]
    slot = jnp.arange(SLOTS, dtype=jnp.int32)
    rank = jnp.sum(
        ((receiver[:, None] == receiver[None, :]) & (slot[None, :] < slot[:, None])).astype(jnp.int32), axis=1
    )
    to_row, to_col = receiver // N_PHI, receiver % N_PHI
    end_spot = 2 * (to_col % 2) + rank
    spot = jnp.where(
        to_row == 0, end_spot, jnp.where(to_row == N_THETA - 1, PARCEL - 4 + end_spot, 2 + 2 * to_row + rank)
    )
    place = jnp.where(to_col // 2 == pi // 2, spot, PARCEL + spot)
    core = (pi % 2).astype(jnp.int32).reshape(1)

    def across(x, by):
        pairs = [(a * N_PHI + p, (1 - a) * N_PHI + (p + by) % N_PHI) for a in range(2) for p in range(N_PHI)]
        return lax.ppermute(x, ("patch", "phi"), pairs)

    def gather_pair(near, far):
        near, far = across(near, 0), across(far, 2)
        swap = [(0, 1), (1, 0), (2, 3), (3, 2)]
        return near, far, lax.ppermute(near, "phi", swap), lax.ppermute(far, "phi", swap)

    def exchange(near, far, *first):
        chunks = run_sort(*gather_pair(near, far), core)
        chunks, first = lax.optimization_barrier((chunks, first))
        chunks = chunks.reshape(N_THETA, CHUNK * FIELDS, SHELLS)
        moved = lax.all_to_all(chunks, "theta", 0, 0, tiled=True)
        return moved.reshape(N_THETA * CHUNK, FIELDS, SHELLS), *first

    def exchange_ids(sent):
        lanes = [jnp.pad(sent[n * PARCEL : (n + 1) * PARCEL], (0, SHELLS - PARCEL))[None] for n in range(2)]
        own = jnp.concatenate([across(lanes[0], 0), across(lanes[1], 2)])
        parts = jnp.concatenate([own, lax.ppermute(own, "phi", [(0, 1), (1, 0), (2, 3), (3, 2)])])
        inside = parts[:, 4 : PARCEL - 4].reshape(4, N_THETA - 2, 2)
        first = lax.dynamic_slice_in_dim(parts, 2 * core[0], 2, 1)[:, None]
        final = lax.dynamic_slice_in_dim(parts, PARCEL - 4 + 2 * core[0], 2, 1)[:, None]
        chunks = jnp.concatenate([first, inside, final], axis=1).swapaxes(0, 1).reshape(N_THETA, 1, CHUNK)
        chunks = jnp.pad(chunks, ((0, 0), (0, 0), (0, SHELLS - CHUNK)))
        moved = lax.all_to_all(chunks, "theta", 0, 0, tiled=True)
        return moved[:, 0, :CHUNK].reshape(N_THETA * CHUNK)

    position = jnp.arange(2 * PARCEL, dtype=jnp.int32)
    target = target_cell[0, 0, 0]
    sent = jnp.sum(jnp.where(position[:, None] == place[None, :], target[None, :] + 1, 0), axis=1) - 1
    sent, _ = lax.optimization_barrier((sent, (before, after)))
    ids = jnp.where(jnp.sum(edge) > 0, exchange_ids(sent), -1)
    picked = ids[None, :] == jnp.arange(CELLS, dtype=jnp.int32)[:, None]
    pick = picked.astype(jnp.bfloat16)
    count = jnp.sum(picked.astype(jnp.float32), axis=1)
    mean = jnp.where(count > 0.0, 1.0 / jnp.maximum(count, 1.0), 0.0)
    mean = jnp.broadcast_to(mean[:, None], (CELLS, SHELLS))

    edge, pick = lax.optimization_barrier((edge, pick))
    tail = (edge, row_const, phi_const, inv_r, corner, angle, place)
    block, *pieces, near, far = run_step(False, (above, below, own, before, after, *tail))
    above_west, above_east = [shift(x, "theta", N_THETA, 1) for x in pieces[2:]]
    below_west, below_east = [shift(x, "theta", N_THETA, -1) for x in pieces[:2]]
    moved, above_west, below_west = exchange(near, far, above_west, below_west)
    block, west, east, head, foot = run_merge(False, block, moved, pick, mean)
    fixes = shift(foot, "theta", N_THETA, 1), shift(head, "theta", N_THETA, -1)
    before, after = shift(east, "phi", N_PHI, 1), shift(west, "phi", N_PHI, -1)
    halo = (above_west, above_east, below_west, below_east)
    block, near, far = run_step(True, (*fixes, block, *halo, own, before, after, *tail))
    (result,) = run_merge(True, block, *exchange(near, far), pick, mean)
    return result[None]


def solution(mesh):
    placed = (
        P("patch", None, "theta", "phi", None),
        P("patch", "theta", "phi", None),
        P("patch", "theta", "phi", None, None),
        P("patch", "theta", "phi", None),
        P("patch", "theta", "phi", None),
        P("patch", "theta", "phi", None),
    )
    return jax.shard_map(
        local,
        mesh=mesh,
        in_specs=placed,
        out_specs=P("patch", None, "theta", "phi", None),
        check_vma=False,
    )
```
